256 devices in a mesh: pipe: 4 (over z_lo), dp: 64 (over y, z_hi, x, core).
Axes of the slice: x: 4, y: 4, z: 8 (z_hi: 2, z_lo: 4; z = z_hi * 4 + z_lo), core: 2. Of those that a mesh axis runs over, the one named last changes fastest.
Arguments:
- tokens: bfloat16 [8192, 2560], P('dp'), may hold values from -20 to 20
- cotangent: bfloat16 [8192, 2560], P('dp'), may hold values from -20 to 20
- norm_gain: float32 [4, 2560], P('pipe'), may hold values from 0.1 to 1.9
- norm_bias: float32 [4, 2560], P('pipe'), may hold values from -3 to 3
- proj_weight: bfloat16 [4, 2560, 2560], P('pipe', 'dp'), may hold values from -0.125 to 0.125
Outputs:
- a_inverse: float32 [4, 20, 128, 128], P('pipe')
- g_inverse: float32 [4, 20, 128, 128], P('pipe')
The draws below stay inside these ranges and needn't reach their ends.
All inputs are finite; a program needn't handle non-finite values.
Results may differ from the reference program's by a relative error of at most 0.0028.
Values may be sent and summed in bfloat16 or wider, within the bound.
A program may use at most 64 MiB of HBM per device.

```python
import jax
import jax.numpy as jnp
from jax import lax

D = 2560
BLK = 128
NB = 20
LAYERS = 4
TOKENS = 8192


def banded_rows(base, row_scale, cols, first_off, first_coef, second_off, second_coef):
    mixed = base[:, :cols] + first_coef * base[:, first_off:first_off + cols] + second_coef * base[:, second_off:second_off + cols]
    norm = (1.0 + first_coef * first_coef + second_coef * second_coef) ** 0.5
    return mixed / norm * row_scale


def draw_tokens(key, part):
    key = jax.random.fold_in(key, 11)
    first = jax.random.fold_in(key, 0)
    rising = 1.0 + 2.0 * jnp.arange(TOKENS, dtype=jnp.float32)[:, None] / TOKENS
    base = jax.random.truncated_normal(first, -4.0, 4.0, (TOKENS, D + 8), jnp.float32)
    row_scale = rising
    return banded_rows(base, row_scale, D, 1, 0.7, 5, 0.5).astype(jnp.bfloat16)


def draw_cotangent(key, part):
    key = jax.random.fold_in(key, 12)
    first = jax.random.fold_in(key, 0)
    rising = 1.0 + 2.0 * jnp.arange(TOKENS, dtype=jnp.float32)[:, None] / TOKENS
    base = jax.random.truncated_normal(first, -4.0, 4.0, (TOKENS, D + 8), jnp.float32)
    row_scale = rising
    return banded_rows(base, row_scale, D, 2, 0.6, 7, -0.4).astype(jnp.bfloat16)


def levels(stream_key, dims, shards, least, largest):
    def one(position, blocks):
        steps = jax.random.uniform(jax.random.fold_in(jax.random.fold_in(stream_key, 6), position), (blocks,), jnp.float32, least / len(shards), largest / len(shards))
        return jnp.repeat(jnp.exp(steps), dims[position] // blocks).reshape((-1,) + (1,) * (len(dims) - position - 1))

    factor_of = one(*shards[0])
    for cut in shards[1:]:
        factor_of = factor_of * one(*cut)
    return factor_of


def scatter_about(rng, extent, scale, most, cuts=(), kind=jnp.bfloat16):
    level = levels(rng, extent, cuts, -0.22, 0.18) if cuts else 1.0
    array = jax.random.normal(rng, extent, jnp.float32) * scale * level
    return jnp.minimum(jnp.maximum(array, -most), most).astype(kind)


def setup_inputs(seed: int = 0) -> dict:
    arg_keys = jax.random.split(jax.random.key(seed), 6)
    tokens = draw_tokens(jax.random.fold_in(arg_keys[5], 71), 0)
    cotangent = draw_cotangent(jax.random.fold_in(arg_keys[5], 71), 0)
    norm_gain = jnp.clip(1.0 + 0.18 * jax.random.normal(arg_keys[2], (LAYERS, D), jnp.float32), 0.1, 1.9)
    norm_bias = scatter_about(arg_keys[3], (LAYERS, D), 0.5, 3.0, ((0, 4),), jnp.float32)
    proj_weight = scatter_about(arg_keys[4], (LAYERS, D, D), D ** -0.5, 0.125, ((0, 4), (1, 64)))
    return dict(tokens=tokens, cotangent=cotangent, norm_gain=norm_gain, norm_bias=norm_bias, proj_weight=proj_weight)


def norm_part(xf, gain, bias):
    mean = lax.optimization_barrier(jnp.mean(xf, axis=-1, keepdims=True))
    centered = xf - mean
    var = lax.optimization_barrier(jnp.mean(centered * centered, axis=-1, keepdims=True))
    return centered * lax.rsqrt(var + 1e-05) * gain + bias

def gelu_tanh(value):
    return jax.nn.gelu(value, approximate=True)

def gram_blocks(rows):

    def one_block(index):
        piece = lax.dynamic_slice_in_dim(rows, index * BLK, BLK, 1)
        return jnp.dot(piece.T.astype(jnp.float32), piece.astype(jnp.float32), preferred_element_type=jnp.float32)
    return lax.map(one_block, jnp.arange(NB, dtype=jnp.int32)) / float(TOKENS)

def invert(block):
    eye = jnp.eye(block.shape[0], dtype=block.dtype)
    damping = 0.1 * jnp.mean(jnp.diagonal(block))
    lower = jnp.linalg.cholesky(block + damping * eye)
    inner = lax.linalg.triangular_solve(lower, eye, left_side=True, lower=True)
    return lax.linalg.triangular_solve(lower, inner, left_side=True, lower=True, transpose_a=True)

def reference(tokens, cotangent, norm_gain, norm_bias, proj_weight):
    current = tokens
    inputs = []
    preacts = []
    a_list = []
    for layer in range(LAYERS):
        inputs.append(current)
        xf = current.astype(jnp.float32)
        hidden = norm_part(xf, norm_gain[layer], norm_bias[layer]).astype(jnp.bfloat16)
        preact = jnp.dot(hidden.astype(jnp.float32), proj_weight[layer].astype(jnp.float32), preferred_element_type=jnp.float32)
        preacts.append(preact)
        current = (xf + gelu_tanh(preact)).astype(jnp.bfloat16)
        a_list.append(jax.vmap(invert)(gram_blocks(hidden)))
    grad = cotangent
    g_list = [None] * LAYERS
    for layer in reversed(range(LAYERS)):
        grad_f = grad.astype(jnp.float32)
        _, pull_gelu = jax.vjp(gelu_tanh, preacts[layer])
        grad_u = pull_gelu(grad_f)[0].astype(jnp.bfloat16)
        g_list[layer] = jax.vmap(invert)(gram_blocks(grad_u))
        grad_h = jnp.dot(grad_u.astype(jnp.float32), proj_weight[layer].T.astype(jnp.float32), preferred_element_type=jnp.float32)
        xf = inputs[layer].astype(jnp.float32)
        gain = norm_gain[layer]
        bias = norm_bias[layer]
        _, pull_norm = jax.vjp(lambda v: norm_part(v, gain, bias), xf)
        grad = (grad_f + pull_norm(grad_h)[0]).astype(jnp.bfloat16)
    return (jnp.stack(a_list), jnp.stack(g_list))
```

```python
import functools
import jax
import jax.numpy as jnp
from jax import lax
from jax.experimental import pallas as pl
from jax.experimental.pallas import tpu as pltpu
from jax.sharding import PartitionSpec as P

BLK = 128
MICRO = 4
F32 = jnp.float32


def wrap4(value):
    return lax.rem(value + 4, 4)


def sweep_inverse(m_ref, count):
    lane8 = lax.broadcasted_iota(jnp.int32, (8, BLK), 1)
    sub8 = lax.broadcasted_iota(jnp.int32, (8, BLK), 0)
    lane_full = lax.broadcasted_iota(jnp.int32, (BLK, BLK), 1)

    def step(kb, carry):
        base = pl.multiple_of(kb * 8, 8)
        in_block = lane8 // 8 == kb
        in_block_full = lane_full // 8 == kb
        select = jnp.where(lane8 == base + sub8, 1.0, 0.0).astype(F32)
        rows = [m_ref[j, pl.ds(base, 8), :] for j in range(count)]
        work = [pltpu.roll(row, lax.rem(BLK - base, BLK), axis=1) for row in rows]
        for i in range(8):
            for j in range(count):
                panel = work[j]
                inv = 1.0 / panel[i : i + 1, i : i + 1]
                col = panel[:, i : i + 1]
                scaled = jnp.where(lane8[:1] == i, inv, panel[i : i + 1, :] * inv)
                rest = jnp.where(lane8 == i, 0.0, panel) - col * scaled
                work[j] = jnp.where(sub8 == i, scaled, rest)
        for j in range(count):
            solved = pltpu.roll(work[j], base, axis=1)
            outside = jnp.where(in_block, 0.0, solved)
            left = jnp.concatenate([jnp.where(in_block, 0.0, rows[j]), outside], axis=0)
            right = jnp.concatenate([-outside, select], axis=0)
            update = lax.dot_general(
                left, right, (((0,), (0,)), ((), ())),
                precision=lax.Precision.HIGHEST, preferred_element_type=F32,
            )
            m_ref[j] = jnp.where(in_block_full, 0.0, m_ref[j]) + update
            m_ref[j, pl.ds(base, 8), :] = outside - jnp.where(in_block, solved, 0.0)
        return carry

    lax.fori_loop(0, BLK // 8, step, 0)


def factor_kernel(
    total, parts, out, from_core, summed, half_l, half_r, full_l, full_r,
    part_hl, part_hr, part_l, part_r, mine, from_z, gathered, final, send_sem, recv_sem,
):
    me = lax.axis_index("dp")
    core = lax.rem(me, 2)
    x = lax.rem(me // 2, 4)
    z = lax.rem(me // 8, 2)
    y = me // 16
    p1 = x + core * (y - x)
    p2 = y + core * (x - y)
    stride1 = 2 + 14 * core
    stride2 = 16 - 14 * core
    right1 = me + (wrap4(p1 + 1) - p1) * stride1
    left1 = me + (wrap4(p1 - 1) - p1) * stride1
    right2 = me + (wrap4(p2 + 1) - p2) * stride2
    left2 = me + (wrap4(p2 - 1) - p2) * stride2
    across = me + (1 - 2 * z) * 8
    sibling = me + 1 - 2 * core

    def copy(index, src, dst, device):
        return pltpu.make_async_remote_copy(
            src_ref=src, dst_ref=dst, send_sem=send_sem.at[index], recv_sem=recv_sem.at[index],
            device_id={"dp": device}, device_id_type=pl.DeviceIdType.MESH,
        )

    barrier = pltpu.get_barrier_semaphore()
    for device in (sibling, right1, left1, right2, left2, across):
        pl.semaphore_signal(
            barrier, inc=1, device_id={"dp": device}, device_id_type=pl.DeviceIdType.MESH
        )
    pl.semaphore_wait(barrier, 6)

    other = 1 - core
    theirs = [wrap4(p2 + 2), wrap4(p2 + 1), wrap4(p2 - 1), p2]
    ours = [wrap4(p1 + 2), wrap4(p1 + 1), wrap4(p1 - 1), p1]
    started = []

    def start(index, src, dst, device):
        item = copy(index, src, dst, device)
        item.start()
        started.append(item)

    for k in range(4):
        start(k, parts.at[other, theirs[k]], from_core.at[theirs[k]], sibling)

    def arrive_core(k):
        group = ours[k]
        copy(k, from_core.at[group], from_core.at[group], sibling).wait_recv()
        summed[group] = parts[core, group] + from_core[group]

    opp, right, left, own = ours
    half = BLK // 2
    lo, hi = pl.ds(0, half), pl.ds(half, half)
    arrive_core(0)
    start(4, summed.at[opp, :, lo], half_l, right1)
    start(5, summed.at[opp, :, hi], half_r, left1)
    arrive_core(1)
    copy(4, half_l, half_l, left1).wait_recv()
    summed[right, :, lo] += half_l[...]
    start(6, summed.at[right], full_l, right1)
    arrive_core(2)
    copy(5, half_r, half_r, right1).wait_recv()
    summed[left, :, hi] += half_r[...]
    start(7, summed.at[left], full_r, left1)
    arrive_core(3)
    copy(6, full_l, full_l, left1).wait_recv()
    copy(7, full_r, full_r, right1).wait_recv()
    gathered[...] = (summed[own] + full_l[...]) + full_r[...]

    quarter, eighth = BLK // 4, BLK // 8

    def rows(part, offset=0, size=quarter):
        return pl.ds(pl.multiple_of(part * quarter + offset, eighth), size)

    opp2, right_2, left_2 = wrap4(p2 + 2), wrap4(p2 + 1), wrap4(p2 - 1)
    start(8, gathered.at[:, rows(opp2, 0, eighth)], part_hl, right2)
    start(9, gathered.at[:, rows(opp2, eighth, eighth)], part_hr, left2)
    copy(8, part_hl, part_hl, left2).wait_recv()
    gathered[:, rows(right_2, 0, eighth)] += part_hl[...]
    start(10, gathered.at[:, rows(right_2)], part_l, right2)
    copy(9, part_hr, part_hr, right2).wait_recv()
    gathered[:, rows(left_2, eighth, eighth)] += part_hr[...]
    start(11, gathered.at[:, rows(left_2)], part_r, left2)
    copy(10, part_l, part_l, left2).wait_recv()
    copy(11, part_r, part_r, right2).wait_recv()
    mine[...] = (gathered[:, rows(p2)] + part_l[...]) + part_r[...]

    start(12, mine, from_z, across)
    copy(12, from_z, from_z, across).wait_recv()
    scale = 1.0 / total
    final[:, rows(p2)] = (mine[...] + from_z[...]) * scale

    start(13, final.at[:, rows(p2)], final.at[:, rows(p2)], right2)
    start(14, final.at[:, rows(p2)], final.at[:, rows(p2)], left2)
    copy(13, final.at[:, rows(left_2)], final.at[:, rows(left_2)], left2).wait_recv()
    start(15, final.at[:, rows(left_2, 0, eighth)], final.at[:, rows(left_2, 0, eighth)], right2)
    copy(14, final.at[:, rows(right_2)], final.at[:, rows(right_2)], right2).wait_recv()
    start(
        16, final.at[:, rows(right_2, eighth, eighth)],
        final.at[:, rows(right_2, eighth, eighth)], left2,
    )
    copy(15, part_hl, final.at[:, rows(opp2, 0, eighth)], left2).wait_recv()
    copy(16, part_hr, final.at[:, rows(opp2, eighth, eighth)], right2).wait_recv()
    for item in started[-4:]:
        item.wait_send()

    count = final.shape[0]
    diagonal = lax.broadcasted_iota(jnp.int32, (BLK, BLK), 0) == lax.broadcasted_iota(
        jnp.int32, (BLK, BLK), 1
    )
    for j in range(count):
        block = final[j]
        on_diagonal = jnp.where(diagonal, block, 0.0)
        trace = jnp.sum(jnp.sum(on_diagonal, axis=0, keepdims=True), axis=1, keepdims=True)
        final[j] = block + jnp.where(diagonal, trace * (0.1 / BLK), 0.0)
    sweep_inverse(final, count)
    out[core, p1] = -final[...]

    start(17, out.at[core, own], out.at[core, own], right1)
    start(18, out.at[core, own], out.at[core, own], left1)
    start(21, out.at[core, own], out.at[core, own], sibling)
    copy(17, out.at[core, left], out.at[core, left], left1).wait_recv()
    start(19, out.at[core, left, :, lo], out.at[core, left, :, lo], right1)
    start(22, out.at[core, left], out.at[core, left], sibling)
    copy(18, out.at[core, right], out.at[core, right], right1).wait_recv()
    start(20, out.at[core, right, :, hi], out.at[core, right, :, hi], left1)
    start(23, out.at[core, right], out.at[core, right], sibling)
    copy(19, half_l, out.at[core, opp, :, lo], left1).wait_recv()
    copy(20, half_r, out.at[core, opp, :, hi], right1).wait_recv()
    start(24, out.at[core, opp], out.at[core, opp], sibling)
    for k, group in enumerate((p2, wrap4(p2 - 1), wrap4(p2 + 1), wrap4(p2 + 2))):
        copy(21 + k, out.at[other, group], out.at[other, group], sibling).wait_recv()
    for item in started[:13] + started[17:]:
        item.wait_send()


def invert_factors(parts, total):
    blocks = parts.shape[1]
    group = blocks // 4
    spec = pl.BlockSpec(memory_space=pltpu.VMEM)
    result = pl.pallas_call(
        functools.partial(factor_kernel, total),
        out_shape=jax.ShapeDtypeStruct((2, 4, group, BLK, BLK), F32),
        in_specs=[spec],
        out_specs=spec,
        scratch_shapes=[
            pltpu.VMEM((4, group, BLK, BLK), F32),
            pltpu.VMEM((4, group, BLK, BLK), F32),
            pltpu.VMEM((group, BLK // 2, BLK), F32),
            pltpu.VMEM((group, BLK // 2, BLK), F32),
            pltpu.VMEM((group, BLK, BLK), F32),
            pltpu.VMEM((group, BLK, BLK), F32),
            pltpu.VMEM((group, BLK // 8, BLK), F32),
            pltpu.VMEM((group, BLK // 8, BLK), F32),
            pltpu.VMEM((group, BLK // 4, BLK), F32),
            pltpu.VMEM((group, BLK // 4, BLK), F32),
            pltpu.VMEM((group, BLK // 4, BLK), F32),
            pltpu.VMEM((group, BLK // 4, BLK), F32),
            pltpu.VMEM((group, BLK, BLK), F32),
            pltpu.VMEM((group, BLK, BLK), F32),
            pltpu.SemaphoreType.DMA((25,)),
            pltpu.SemaphoreType.DMA((25,)),
        ],
        compiler_params=pltpu.CompilerParams(
            collective_id=0, has_side_effects=True, vmem_limit_bytes=40 * 1024 * 1024
        ),
    )(parts.reshape(2, 4, group, BLK, BLK))
    return result.reshape(2, blocks, BLK, BLK)


def shifted(array, axis, by):
    count = lax.axis_size(axis)
    pairs = [(i, i + by) for i in range(count) if 0 <= i + by < count]
    return lax.ppermute(array, axis, pairs)


def norm_part(xf, gain, bias):
    mean = jnp.mean(xf, axis=-1, keepdims=True)
    centered = xf - mean
    var = jnp.mean(centered * centered, axis=-1, keepdims=True)
    return centered * lax.rsqrt(var + 1e-05) * gain + bias


def gelu_tanh(value):
    return jax.nn.gelu(value, approximate=True)


def local_grams(stored, rows, width):
    blocks = stored.reshape(rows, width // BLK, BLK)
    return jnp.einsum("tjb,tjc->jbc", blocks, blocks, preferred_element_type=jnp.float32)


def store_at(buffer, value, index, valid):
    kept = jnp.where(valid, value, buffer[index])
    return lax.dynamic_update_index_in_dim(buffer, kept, index, 0)


def per_device(tokens, cotangent, norm_gain, norm_bias, proj_weight):
    sections = lax.axis_size("pipe")
    section = lax.axis_index("pipe")
    replicas = lax.axis_size("dp")
    rows, width = tokens.shape
    mrows = rows // MICRO
    gain = norm_gain[0]
    bias = norm_bias[0]
    full_weight = lax.all_gather(proj_weight[0], "dp", axis=0, tiled=True)
    tok_blocks = tokens.reshape(MICRO, mrows, width)
    cot_blocks = cotangent.reshape(MICRO, mrows, width)
    inputs = jnp.zeros((MICRO, mrows, width), jnp.bfloat16)
    preacts = jnp.zeros((MICRO, mrows, width), jnp.float32)
    activations = jnp.zeros((MICRO, mrows, width), jnp.bfloat16)
    gradients = jnp.zeros((MICRO, mrows, width), jnp.bfloat16)
    received = jnp.zeros((mrows, width), jnp.bfloat16)
    for tick in range(MICRO + sections - 1):
        micro = tick - section
        valid = (micro >= 0) & (micro < MICRO)
        index = jnp.clip(micro, 0, MICRO - 1)
        current = jnp.where(section == 0, tok_blocks[index], received)
        xf = current.astype(jnp.float32)
        hidden = norm_part(xf, gain, bias).astype(jnp.bfloat16)
        preact = jnp.dot(hidden, full_weight, preferred_element_type=jnp.float32)
        out = (xf + gelu_tanh(preact)).astype(jnp.bfloat16)
        inputs = store_at(inputs, current, index, valid)
        preacts = store_at(preacts, preact, index, valid)
        activations = store_at(activations, hidden, index, valid)
        received = shifted(out, "pipe", 1)
    received = jnp.zeros((mrows, width), jnp.bfloat16)
    for tick in range(MICRO + sections - 1):
        micro = tick - (sections - 1 - section)
        valid = (micro >= 0) & (micro < MICRO)
        index = jnp.clip(micro, 0, MICRO - 1)
        grad_out = jnp.where(section == sections - 1, cot_blocks[index], received)
        grad_f = grad_out.astype(jnp.float32)
        _, pull_gelu = jax.vjp(gelu_tanh, preacts[index])
        grad_u = pull_gelu(grad_f)[0].astype(jnp.bfloat16)
        gradients = store_at(gradients, grad_u, index, valid)
        grad_h = lax.dot_general(
            grad_u, full_weight, (((1,), (1,)), ((), ())), preferred_element_type=jnp.float32
        )
        xf = inputs[index].astype(jnp.float32)
        _, pull_norm = jax.vjp(lambda v: norm_part(v, gain, bias), xf)
        grad_in = (grad_f + pull_norm(grad_h)[0]).astype(jnp.bfloat16)
        received = shifted(grad_in, "pipe", -1)
    a_part = local_grams(activations, rows, width)
    g_part = local_grams(gradients, rows, width)
    total = float(rows * replicas)
    inverses = invert_factors(jnp.stack([a_part, g_part]), total)
    return (inverses[:1], inverses[1:])


def solution(mesh):
    in_specs = (
        P("dp", None),
        P("dp", None),
        P("pipe", None),
        P("pipe", None),
        P("pipe", "dp", None),
    )
    out_specs = (P("pipe", None, None, None), P("pipe", None, None, None))
    return jax.shard_map(
        per_device, mesh=mesh, in_specs=in_specs, out_specs=out_specs, check_vma=False
    )
```

```python
import functools
import jax
import jax.numpy as jnp
from jax import lax
from jax.experimental import pallas as pl
from jax.experimental.pallas import tpu as pltpu
from jax.sharding import PartitionSpec as P

BLK = 128
TILE = 256
MICRO = 4
SLOPE = (2.0 / 3.141592653589793) ** 0.5
CUBIC = 0.044715
F32 = jnp.float32


def wrap4(value):
    return lax.rem(value + 4, 4)


def sweep_inverse(m_ref, count):
    lane8 = lax.broadcasted_iota(jnp.int32, (8, BLK), 1)
    sub8 = lax.broadcasted_iota(jnp.int32, (8, BLK), 0)
    lane_full = lax.broadcasted_iota(jnp.int32, (BLK, BLK), 1)

    def step(kb, carry):
        base = pl.multiple_of(kb * 8, 8)
        in_block = lane8 // 8 == kb
        in_block_full = lane_full // 8 == kb
        select = jnp.where(lane8 == base + sub8, 1.0, 0.0).astype(F32)
        rows = [m_ref[j, pl.ds(base, 8), :] for j in range(count)]
        work = [pltpu.roll(row, lax.rem(BLK - base, BLK), axis=1) for row in rows]
        for i in range(8):
            for j in range(count):
                panel = work[j]
                inv = 1.0 / panel[i : i + 1, i : i + 1]
                col = panel[:, i : i + 1]
                scaled = jnp.where(lane8[:1] == i, inv, panel[i : i + 1, :] * inv)
                rest = jnp.where(lane8 == i, 0.0, panel) - col * scaled
                work[j] = jnp.where(sub8 == i, scaled, rest)
        for j in range(count):
            solved = pltpu.roll(work[j], base, axis=1)
            outside = jnp.where(in_block, 0.0, solved)
            left = jnp.concatenate([jnp.where(in_block, 0.0, rows[j]), outside], axis=0)
            right = jnp.concatenate([-outside, select], axis=0)
            update = lax.dot_general(
                left, right, (((0,), (0,)), ((), ())),
                precision=lax.Precision.HIGHEST, preferred_element_type=F32,
            )
            m_ref[j] = jnp.where(in_block_full, 0.0, m_ref[j]) + update
            m_ref[j, pl.ds(base, 8), :] = outside - jnp.where(in_block, solved, 0.0)
        return carry

    lax.fori_loop(0, BLK // 8, step, 0)


def factor_kernel(
    total, parts, out, from_core, summed, half_l, half_r, full_l, full_r,
    part_hl, part_hr, part_l, part_r, mine, from_z, gathered, final, send_sem, recv_sem,
):
    me = lax.axis_index("dp")
    core = lax.rem(me, 2)
    x = lax.rem(me // 2, 4)
    z = lax.rem(me // 8, 2)
    y = me // 16
    p1 = x + core * (y - x)
    p2 = y + core * (x - y)
    stride1 = 2 + 14 * core
    stride2 = 16 - 14 * core
    right1 = me + (wrap4(p1 + 1) - p1) * stride1
    left1 = me + (wrap4(p1 - 1) - p1) * stride1
    right2 = me + (wrap4(p2 + 1) - p2) * stride2
    left2 = me + (wrap4(p2 - 1) - p2) * stride2
    across = me + (1 - 2 * z) * 8
    sibling = me + 1 - 2 * core

    def copy(index, src, dst, device):
        return pltpu.make_async_remote_copy(
            src_ref=src, dst_ref=dst, send_sem=send_sem.at[index], recv_sem=recv_sem.at[index],
            device_id={"dp": device}, device_id_type=pl.DeviceIdType.MESH,
        )

    barrier = pltpu.get_barrier_semaphore()
    for device in (sibling, right1, left1, right2, left2, across):
        pl.semaphore_signal(
            barrier, inc=1, device_id={"dp": device}, device_id_type=pl.DeviceIdType.MESH
        )
    pl.semaphore_wait(barrier, 6)

    other = 1 - core
    theirs = [wrap4(p2 + 2), wrap4(p2 + 1), wrap4(p2 - 1), p2]
    ours = [wrap4(p1 + 2), wrap4(p1 + 1), wrap4(p1 - 1), p1]
    started = []

    def start(index, src, dst, device):
        item = copy(index, src, dst, device)
        item.start()
        started.append(item)

    for k in range(4):
        start(k, parts.at[other, theirs[k]], from_core.at[theirs[k]], sibling)

    def arrive_core(k):
        group = ours[k]
        copy(k, from_core.at[group], from_core.at[group], sibling).wait_recv()
        summed[group] = parts[core, group] + from_core[group]

    opp, right, left, own = ours
    half = BLK // 2
    lo, hi = pl.ds(0, half), pl.ds(half, half)
    arrive_core(0)
    start(4, summed.at[opp, :, lo], half_l, right1)
    start(5, summed.at[opp, :, hi], half_r, left1)
    arrive_core(1)
    copy(4, half_l, half_l, left1).wait_recv()
    summed[right, :, lo] += half_l[...]
    start(6, summed.at[right], full_l, right1)
    arrive_core(2)
    copy(5, half_r, half_r, right1).wait_recv()
    summed[left, :, hi] += half_r[...]
    start(7, summed.at[left], full_r, left1)
    arrive_core(3)
    copy(6, full_l, full_l, left1).wait_recv()
    copy(7, full_r, full_r, right1).wait_recv()
    gathered[...] = (summed[own] + full_l[...]) + full_r[...]

    quarter, eighth = BLK // 4, BLK // 8

    def rows(part, offset=0, size=quarter):
        return pl.ds(pl.multiple_of(part * quarter + offset, eighth), size)

    opp2, right_2, left_2 = wrap4(p2 + 2), wrap4(p2 + 1), wrap4(p2 - 1)
    start(8, gathered.at[:, rows(opp2, 0, eighth)], part_hl, right2)
    start(9, gathered.at[:, rows(opp2, eighth, eighth)], part_hr, left2)
    copy(8, part_hl, part_hl, left2).wait_recv()
    gathered[:, rows(right_2, 0, eighth)] += part_hl[...]
    start(10, gathered.at[:, rows(right_2)], part_l, right2)
    copy(9, part_hr, part_hr, right2).wait_recv()
    gathered[:, rows(left_2, eighth, eighth)] += part_hr[...]
    start(11, gathered.at[:, rows(left_2)], part_r, left2)
    copy(10, part_l, part_l, left2).wait_recv()
    copy(11, part_r, part_r, right2).wait_recv()
    mine[...] = (gathered[:, rows(p2)] + part_l[...]) + part_r[...]

    start(12, mine, from_z, across)
    copy(12, from_z, from_z, across).wait_recv()
    scale = 1.0 / total
    final[:, rows(p2)] = (mine[...] + from_z[...]) * scale

    start(13, final.at[:, rows(p2)], final.at[:, rows(p2)], right2)
    start(14, final.at[:, rows(p2)], final.at[:, rows(p2)], left2)
    copy(13, final.at[:, rows(left_2)], final.at[:, rows(left_2)], left2).wait_recv()
    start(15, final.at[:, rows(left_2, 0, eighth)], final.at[:, rows(left_2, 0, eighth)], right2)
    copy(14, final.at[:, rows(right_2)], final.at[:, rows(right_2)], right2).wait_recv()
    start(
        16, final.at[:, rows(right_2, eighth, eighth)],
        final.at[:, rows(right_2, eighth, eighth)], left2,
    )
    copy(15, part_hl, final.at[:, rows(opp2, 0, eighth)], left2).wait_recv()
    copy(16, part_hr, final.at[:, rows(opp2, eighth, eighth)], right2).wait_recv()
    for item in started[-4:]:
        item.wait_send()

    count = final.shape[0]
    diagonal = lax.broadcasted_iota(jnp.int32, (BLK, BLK), 0) == lax.broadcasted_iota(
        jnp.int32, (BLK, BLK), 1
    )
    for j in range(count):
        block = final[j]
        on_diagonal = jnp.where(diagonal, block, 0.0)
        trace = jnp.sum(jnp.sum(on_diagonal, axis=0, keepdims=True), axis=1, keepdims=True)
        final[j] = block + jnp.where(diagonal, trace * (0.1 / BLK), 0.0)
    sweep_inverse(final, count)
    out[core, p1] = -final[...]

    start(17, out.at[core, own], out.at[core, own], right1)
    start(18, out.at[core, own], out.at[core, own], left1)
    start(21, out.at[core, own], out.at[core, own], sibling)
    copy(17, out.at[core, left], out.at[core, left], left1).wait_recv()
    start(19, out.at[core, left, :, lo], out.at[core, left, :, lo], right1)
    start(22, out.at[core, left], out.at[core, left], sibling)
    copy(18, out.at[core, right], out.at[core, right], right1).wait_recv()
    start(20, out.at[core, right, :, hi], out.at[core, right, :, hi], left1)
    start(23, out.at[core, right], out.at[core, right], sibling)
    copy(19, half_l, out.at[core, opp, :, lo], left1).wait_recv()
    copy(20, half_r, out.at[core, opp, :, hi], right1).wait_recv()
    start(24, out.at[core, opp], out.at[core, opp], sibling)
    for k, group in enumerate((p2, wrap4(p2 - 1), wrap4(p2 + 1), wrap4(p2 + 2))):
        copy(21 + k, out.at[other, group], out.at[other, group], sibling).wait_recv()
    for item in started[:13] + started[17:]:
        item.wait_send()


def invert_factors(parts, total):
    blocks = parts.shape[1]
    group = blocks // 4
    spec = pl.BlockSpec(memory_space=pltpu.VMEM)
    result = pl.pallas_call(
        functools.partial(factor_kernel, total),
        out_shape=jax.ShapeDtypeStruct((2, 4, group, BLK, BLK), F32),
        in_specs=[spec],
        out_specs=spec,
        scratch_shapes=[
            pltpu.VMEM((4, group, BLK, BLK), F32),
            pltpu.VMEM((4, group, BLK, BLK), F32),
            pltpu.VMEM((group, BLK // 2, BLK), F32),
            pltpu.VMEM((group, BLK // 2, BLK), F32),
            pltpu.VMEM((group, BLK, BLK), F32),
            pltpu.VMEM((group, BLK, BLK), F32),
            pltpu.VMEM((group, BLK // 8, BLK), F32),
            pltpu.VMEM((group, BLK // 8, BLK), F32),
            pltpu.VMEM((group, BLK // 4, BLK), F32),
            pltpu.VMEM((group, BLK // 4, BLK), F32),
            pltpu.VMEM((group, BLK // 4, BLK), F32),
            pltpu.VMEM((group, BLK // 4, BLK), F32),
            pltpu.VMEM((group, BLK, BLK), F32),
            pltpu.VMEM((group, BLK, BLK), F32),
            pltpu.SemaphoreType.DMA((25,)),
            pltpu.SemaphoreType.DMA((25,)),
        ],
        compiler_params=pltpu.CompilerParams(
            collective_id=0, has_side_effects=True, vmem_limit_bytes=40 * 1024 * 1024
        ),
    )(parts.reshape(2, 4, group, BLK, BLK))
    return result.reshape(2, blocks, BLK, BLK)


def pipeline_kernel(
    tokens, cotangent, norm_gain, norm_bias, shard, grams, weight, stage, entering, arriving,
    hidden, normed, rstd, slope, gradient, leaving, returning,
    pair_send, pair_recv, z_send, z_recv, ring_send, ring_recv, twin_send, twin_recv,
    next_send, next_recv, prev_send, prev_recv,
):
    me = lax.axis_index("dp")
    section = lax.axis_index("pipe")
    core = lax.rem(me, 2)
    x = lax.rem(me // 2, 4)
    z = lax.rem(me // 8, 2)
    y = me // 16
    p1 = x + core * (y - x)
    p2 = y + core * (x - y)
    stride1 = 2 + 14 * core
    stride2 = 16 - 14 * core
    right1 = me + (wrap4(p1 + 1) - p1) * stride1
    left1 = me + (wrap4(p1 - 1) - p1) * stride1
    right2 = me + (wrap4(p2 + 1) - p2) * stride2
    left2 = me + (wrap4(p2 - 1) - p2) * stride2
    across = me + (1 - 2 * z) * 8
    sibling = me + 1 - 2 * core
    following = wrap4(section + 1)
    previous = wrap4(section - 1)
    micros, mrows, width = entering.shape
    depth = stage.shape[0]
    side = width // 2
    last = section == 3

    def remote(src, dst, send, recv, **device):
        return pltpu.make_async_remote_copy(
            src_ref=src, dst_ref=dst, send_sem=send, recv_sem=recv,
            device_id=device, device_id_type=pl.DeviceIdType.MESH,
        )

    barrier = pltpu.get_barrier_semaphore()
    for device in (sibling, right1, left1, right2, left2, across):
        pl.semaphore_signal(
            barrier, inc=1, device_id={"dp": device}, device_id_type=pl.DeviceIdType.MESH
        )
    for device in (following, previous):
        pl.semaphore_signal(
            barrier, inc=1, device_id={"pipe": device}, device_id_type=pl.DeviceIdType.MESH
        )
    pl.semaphore_wait(barrier, 8)

    mine = pl.ds(pl.multiple_of(core * (depth // 2), 8), depth // 2)
    theirs = pl.ds(pl.multiple_of((1 - core) * (depth // 2), 8), depth // 2)
    pair = remote(shard.at[1 - core], stage.at[mine], pair_send, pair_recv, dp=sibling)
    pair.start()
    stage[mine] = shard[core]
    remote(stage.at[theirs], stage.at[theirs], pair_send, pair_recv, dp=sibling).wait_recv()

    def block(part, a, b, plane, columns=None):
        chip = (a + part * (b - a)) + 4 * plane + 8 * (b + part * (a - b))
        rows = pl.ds(pl.multiple_of(chip * depth, 16), depth)
        if columns is None:
            return weight.at[part, rows]
        return weight.at[part, rows, columns]

    chip = me // 2
    weight[core, pl.ds(pl.multiple_of(chip * depth, 16), depth)] = stage[...].astype(jnp.bfloat16)

    started = []

    def send(slot, ref, device):
        item = remote(ref, ref, ring_send.at[slot], ring_recv.at[slot], dp=device)
        item.start()
        started.append(item)

    def await_block(slot, ref, device):
        remote(ref, ref, ring_send.at[slot], ring_recv.at[slot], dp=device).wait_recv()

    twins = []

    def mirror(slot, a, b, plane):
        ref = block(core, a, b, plane)
        item = remote(ref, ref, twin_send.at[slot], twin_recv.at[slot], dp=sibling)
        item.start()
        twins.append(item)

    own = block(core, p1, p2, z)
    z_copy = remote(own, own, z_send, z_recv, dp=across)
    z_copy.start()

    low, high = pl.ds(0, side // 2), pl.ds(side // 2, side // 2)
    a_order = [p1, wrap4(p1 - 1), wrap4(p1 + 1), wrap4(p1 + 2)]
    b_order = [p2, wrap4(p2 - 1), wrap4(p2 + 1), wrap4(p2 + 2)]
    for turn in range(2):
        plane = z if turn == 0 else 1 - z
        base = 20 * turn
        if turn == 1:
            got = block(core, p1, p2, plane)
            remote(got, got, z_send, z_recv, dp=across).wait_recv()

        def line(i, j, columns=None):
            return block(core, a_order[i], b_order[j], plane, columns)

        def second_start(i):
            send(base + 4 + 4 * i, line(i, 0), right2)
            send(base + 5 + 4 * i, line(i, 0), left2)
            mirror(16 * turn + 4 * i, a_order[i], b_order[0], plane)

        def second_pass(i):
            await_block(base + 4 + 4 * i, line(i, 1), left2)
            send(base + 6 + 4 * i, line(i, 1, low), right2)
            mirror(16 * turn + 4 * i + 1, a_order[i], b_order[1], plane)
            await_block(base + 5 + 4 * i, line(i, 2), right2)
            send(base + 7 + 4 * i, line(i, 2, high), left2)
            mirror(16 * turn + 4 * i + 2, a_order[i], b_order[2], plane)

        def second_end(i):
            await_block(base + 6 + 4 * i, line(i, 3, low), left2)
            await_block(base + 7 + 4 * i, line(i, 3, high), right2)
            mirror(16 * turn + 4 * i + 3, a_order[i], b_order[3], plane)

        send(base, line(0, 0), right1)
        send(base + 1, line(0, 0), left1)
        second_start(0)
        await_block(base, line(1, 0), left1)
        send(base + 2, line(1, 0, low), right1)
        second_start(1)
        await_block(base + 1, line(2, 0), right1)
        send(base + 3, line(2, 0, high), left1)
        second_start(2)
        second_pass(0)
        await_block(base + 2, line(3, 0, low), left1)
        await_block(base + 3, line(3, 0, high), right1)
        second_start(3)
        second_pass(1)
        second_end(0)
        second_pass(2)
        second_end(1)
        second_pass(3)
        second_end(2)
        second_end(3)

    for turn in range(2):
        plane = z if turn == 0 else 1 - z
        for i in range(4):
            for j in range(4):
                ref = block(1 - core, b_order[i], a_order[j], plane)
                slot = 16 * turn + 4 * i + j
                remote(ref, ref, twin_send.at[slot], twin_recv.at[slot], dp=sibling).wait_recv()

    gain = norm_gain[...]
    bias = norm_bias[...]
    tiles = width // TILE

    def tile_of(t):
        return pl.ds(pl.multiple_of(t * TILE, TILE), TILE)

    def half_tile(t):
        half = tiles // 2
        return t // half, pl.ds(pl.multiple_of(lax.rem(t, half) * TILE, TILE), TILE)

    def forward(m, carry):
        @pl.when(section == 0)
        def _():
            entering[m] = tokens[m]

        @pl.when(section > 0)
        def _():
            ref = entering.at[m]
            remote(ref, ref, next_send.at[m], next_recv.at[m], pipe=previous).wait_recv()

        xf = entering[m].astype(F32)
        mean = jnp.mean(xf, axis=-1, keepdims=True)
        centered = xf - mean
        var = jnp.mean(centered * centered, axis=-1, keepdims=True)
        scale = lax.rsqrt(var + 1e-05)
        unit = centered * scale
        normed[m] = unit
        rstd[m] = jnp.broadcast_to(scale, rstd.shape[1:])
        hidden[m] = (unit * gain + bias).astype(jnp.bfloat16)

        def tile(t, inner):
            part, inside = half_tile(t)
            cols = tile_of(t)
            u = jnp.dot(hidden[m], weight[part, :, inside], preferred_element_type=F32)
            square = u * u
            bent = jnp.tanh(SLOPE * (u * (1.0 + CUBIC * square)))
            half = 0.5 * (1.0 + bent)
            slope[m, :, cols] = half + (0.5 * SLOPE) * u * (1.0 - bent * bent) * (
                1.0 + (3.0 * CUBIC) * square
            )
            leaving[m, :, cols] = (entering[m, :, cols].astype(F32) + u * half).astype(jnp.bfloat16)
            return inner

        lax.fori_loop(0, tiles, tile, 0)

        @pl.when(section < 3)
        def _():
            remote(
                leaving.at[m], entering.at[m], next_send.at[m], next_recv.at[m], pipe=following
            ).start()

        return carry

    lax.fori_loop(0, micros, forward, 0)

    def gram(which, rows):
        def one(j, carry):
            cols = pl.ds(pl.multiple_of(j * BLK, BLK), BLK)
            piece = rows[:, :, cols].reshape(micros * mrows, BLK)
            grams[which, j] = lax.dot_general(
                piece, piece, (((0,), (0,)), ((), ())), preferred_element_type=F32
            )
            return carry

        lax.fori_loop(0, width // BLK, one, 0)

    @pl.when(section < 3)
    def _():
        gram(0, hidden)

    def backward(m, carry):
        @pl.when(last)
        def _():
            arriving[m] = cotangent[m]

        @pl.when(section < 3)
        def _():
            ref = arriving.at[m]
            remote(ref, ref, prev_send.at[m], prev_recv.at[m], pipe=following).wait_recv()

        gradient[m] = (slope[m] * arriving[m].astype(F32)).astype(jnp.bfloat16)

        @pl.when(section > 0)
        def _():
            def tile(t, inner):
                rows = tile_of(t)
                back = sum(
                    lax.dot_general(
                        gradient[m, :, part * side : (part + 1) * side], weight[part, rows, :],
                        (((1,), (1,)), ((), ())), preferred_element_type=F32,
                    )
                    for part in range(2)
                )
                slope[m, :, rows] = back * norm_gain[:, rows]
                return inner

            lax.fori_loop(0, tiles, tile, 0)
            back = slope[m]
            unit = normed[m]
            along = jnp.mean(back * unit, axis=-1, keepdims=True)
            level = jnp.mean(back, axis=-1, keepdims=True)
            change = rstd[m, :, :1] * (back - level - unit * along)
            returning[m] = (arriving[m].astype(F32) + change).astype(jnp.bfloat16)
            remote(
                returning.at[m], arriving.at[m], prev_send.at[m], prev_recv.at[m], pipe=previous
            ).start()

        return carry

    lax.fori_loop(0, micros, backward, 0)

    @pl.when(last)
    def _():
        gram(0, hidden)

    gram(1, gradient)

    pair.wait_send()
    z_copy.wait_send()
    for item in started + twins:
        item.wait_send()

    def drain(m, carry):
        @pl.when(section < 3)
        def _():
            remote(
                leaving.at[m], entering.at[m], next_send.at[m], next_recv.at[m], pipe=following
            ).wait_send()

        @pl.when(section > 0)
        def _():
            remote(
                returning.at[m], arriving.at[m], prev_send.at[m], prev_recv.at[m], pipe=previous
            ).wait_send()

        return carry

    lax.fori_loop(0, micros, drain, 0)


def local_factors(tokens, cotangent, norm_gain, norm_bias, proj_weight):
    rows, width = tokens.shape
    depth = 2 * proj_weight.shape[1]
    mrows = rows // MICRO
    shard = proj_weight[0].astype(F32).reshape(depth // 2, 2, width // 2).swapaxes(0, 1)
    by_micro = (MICRO, mrows, width)
    vmem = pl.BlockSpec(memory_space=pltpu.VMEM)
    dma = pltpu.SemaphoreType.DMA
    return pl.pallas_call(
        pipeline_kernel,
        out_shape=jax.ShapeDtypeStruct((2, width // BLK, BLK, BLK), F32),
        in_specs=[vmem] * 5,
        out_specs=vmem,
        scratch_shapes=[
            pltpu.VMEM((2, width, width // 2), jnp.bfloat16),
            pltpu.VMEM((depth, width // 2), F32),
            pltpu.VMEM(by_micro, jnp.bfloat16),
            pltpu.VMEM(by_micro, jnp.bfloat16),
            pltpu.VMEM(by_micro, jnp.bfloat16),
            pltpu.VMEM(by_micro, F32),
            pltpu.VMEM((MICRO, mrows, BLK), F32),
            pltpu.VMEM(by_micro, F32),
            pltpu.VMEM(by_micro, jnp.bfloat16),
            pltpu.VMEM(by_micro, jnp.bfloat16),
            pltpu.VMEM(by_micro, jnp.bfloat16),
            dma, dma, dma, dma, dma((40,)), dma((40,)), dma((32,)), dma((32,)),
            dma((MICRO,)), dma((MICRO,)), dma((MICRO,)), dma((MICRO,)),
        ],
        compiler_params=pltpu.CompilerParams(
            collective_id=1, has_side_effects=True, vmem_limit_bytes=48 * 1024 * 1024
        ),
    )(tokens.reshape(by_micro), cotangent.reshape(by_micro), norm_gain, norm_bias, shard)


def per_device(tokens, cotangent, norm_gain, norm_bias, proj_weight):
    total = float(tokens.shape[0] * lax.axis_size("dp"))
    parts = local_factors(tokens, cotangent, norm_gain, norm_bias, proj_weight)
    inverses = invert_factors(parts, total)
    return (inverses[:1], inverses[1:])


def solution(mesh):
    in_specs = (
        P("dp", None),
        P("dp", None),
        P("pipe", None),
        P("pipe", None),
        P("pipe", "dp", None),
    )
    out_specs = (P("pipe", None, None, None), P("pipe", None, None, None))
    return jax.shard_map(
        per_device, mesh=mesh, in_specs=in_specs, out_specs=out_specs, check_vma=False
    )
```

```python
import functools
import jax
import jax.numpy as jnp
from jax import lax
from jax.experimental import pallas as pl
from jax.experimental.pallas import tpu as pltpu
from jax.sharding import PartitionSpec as P

BLK = 128
PANEL = 16
TILE = 256
MICRO = 4
PIECES = 2
GROUP = 3
COPIES = 25
SLOPE = (2.0 / 3.141592653589793) ** 0.5
CUBIC = 0.044715
F32 = jnp.float32


def wrap4(value):
    return lax.rem(value + 4, 4)


def three_parts(value):
    high = value.astype(jnp.bfloat16)
    rest = value - high.astype(F32)
    middle = rest.astype(jnp.bfloat16)
    low = (rest - middle.astype(F32)).astype(jnp.bfloat16)
    return high, middle, low


def outer_sum(left, right):
    lh, lm, ll = three_parts(left)
    rh, rm, rl = three_parts(right)
    lhs = jnp.concatenate([lh, lh, lm, lh, ll, lm], axis=0)
    rhs = jnp.concatenate([rh, rm, rh, rl, rh, rm], axis=0)
    return lax.dot_general(lhs, rhs, (((0,), (0,)), ((), ())), preferred_element_type=F32)


def sweep_inverse(m_ref):
    count = m_ref.shape[0]
    lane = lax.broadcasted_iota(jnp.int32, (PANEL, BLK), 1)
    row = lax.broadcasted_iota(jnp.int32, (PANEL, BLK), 0)
    lane_full = lax.broadcasted_iota(jnp.int32, (BLK, BLK), 1)
    for base in range(0, BLK, PANEL):
        in_block = lane // PANEL == base // PANEL
        in_block_full = lane_full // PANEL == base // PANEL
        select = jnp.where(lane == base + row, 1.0, 0.0).astype(F32)
        rows = [m_ref[j, base : base + PANEL, :] for j in range(count)]
        work = list(rows)
        columns = [
            [jnp.broadcast_to(panel[:, base + i : base + i + 1], panel.shape) for i in range(PANEL)]
            for panel in rows
        ]
        for i in range(PANEL):
            for j in range(count):
                panel, column = work[j], columns[j]
                inv = 1.0 / column[i][i : i + 1]
                for k in range(i + 1, PANEL):
                    pivot_row = column[k][i : i + 1] * inv
                    column[k] = jnp.where(row == i, pivot_row, column[k] - column[i] * pivot_row)
                scaled = jnp.where(lane[:1] == base + i, inv, panel[i : i + 1] * inv)
                rest = jnp.where(lane == base + i, 0.0, panel) - column[i] * scaled
                work[j] = jnp.where(row == i, scaled, rest)
        for j in range(count):
            solved = work[j]
            outside = jnp.where(in_block, 0.0, solved)
            left = jnp.concatenate([jnp.where(in_block, 0.0, rows[j]), outside], axis=0)
            right = jnp.concatenate([-outside, select], axis=0)
            update = outer_sum(left, right)
            m_ref[j] = jnp.where(in_block_full, 0.0, m_ref[j]) + update
            m_ref[j, base : base + PANEL, :] = outside - jnp.where(in_block, solved, 0.0)


def factor_stages(which, place, remote, total, grams, out, buffers, send_sem, recv_sem):
    core, p1, p2, sibling, right1, left1, right2, left2, across = place
    from_core, summed, half_l, half_r, full_l, full_r, part_hl, part_hr, part_l, part_r, mine, from_z, gathered, final = (
        buffer.at[which] for buffer in buffers
    )
    other = 1 - core
    own, opp, right, left = p1, wrap4(p1 + 2), wrap4(p1 + 1), wrap4(p1 - 1)
    opp2, right_2, left_2 = wrap4(p2 + 2), wrap4(p2 + 1), wrap4(p2 - 1)
    ours, theirs = (opp, right, left, own), (opp2, right_2, left_2, p2)
    half, quarter, eighth = BLK // 2, BLK // 4, BLK // 8
    lo, hi = pl.ds(0, half), pl.ds(half, half)

    def rows(part, offset=0, size=quarter):
        return pl.ds(pl.multiple_of(part * quarter + offset, eighth), size)

    def fin(part, offset=0, size=quarter):
        return final.at[:, rows(part, offset, size)]

    result = out.at[which, core]
    table = [
        (grams.at[which, other, theirs[k]], from_core.at[theirs[k]], sibling, from_core.at[ours[k]])
        for k in range(4)
    ] + [
        (summed.at[opp, :, lo], half_l, right1, half_l),
        (summed.at[opp, :, hi], half_r, left1, half_r),
        (summed.at[right], full_l, right1, full_l),
        (summed.at[left], full_r, left1, full_r),
        (gathered.at[:, rows(opp2, 0, eighth)], part_hl, right2, part_hl),
        (gathered.at[:, rows(opp2, eighth, eighth)], part_hr, left2, part_hr),
        (gathered.at[:, rows(right_2)], part_l, right2, part_l),
        (gathered.at[:, rows(left_2)], part_r, left2, part_r),
        (mine, from_z, across, from_z),
        (fin(p2), fin(p2), right2, fin(left_2)),
        (fin(p2), fin(p2), left2, fin(right_2)),
        (fin(left_2, 0, eighth), fin(left_2, 0, eighth), right2, fin(opp2, 0, eighth)),
        (fin(right_2, eighth, eighth), fin(right_2, eighth, eighth), left2, fin(opp2, eighth, eighth)),
        (result.at[own], result.at[own], right1, result.at[left]),
        (result.at[own], result.at[own], left1, result.at[right]),
        (result.at[left, :, lo], result.at[left, :, lo], right1, result.at[opp, :, lo]),
        (result.at[right, :, hi], result.at[right, :, hi], left1, result.at[opp, :, hi]),
    ] + [
        (result.at[a], result.at[a], sibling, out.at[which, other, b])
        for a, b in zip((own, left, right, opp), (p2, left_2, right_2, opp2))
    ]

    def start(*indices):
        for k in indices:
            src, dst, device, _ = table[k]
            remote(src, dst, send_sem.at[which, k], recv_sem.at[which, k], dp=device).start()

    def received(*indices):
        for k in indices:
            src, _, device, landed = table[k]
            remote(landed, landed, send_sem.at[which, k], recv_sem.at[which, k], dp=device).wait_recv()

    def sent(*indices):
        for k in indices:
            src, dst, device, _ = table[k]
            remote(src, dst, send_sem.at[which, k], recv_sem.at[which, k], dp=device).wait_send()

    def add_core(k):
        received(k)
        summed[ours[k]] = grams[which, core, ours[k]] + from_core[ours[k]]

    def exchange():
        start(0, 1, 2, 3)

    def ring1_first():
        add_core(0)
        start(4, 5)
        add_core(1)
        add_core(2)

    def ring1_second():
        received(4)
        summed[right, :, lo] += half_l[...]
        start(6)
        received(5)
        summed[left, :, hi] += half_r[...]
        start(7)
        add_core(3)

    def ring2_first():
        received(6, 7)
        gathered[...] = (summed[own] + full_l[...]) + full_r[...]
        start(8, 9)

    def ring2_second():
        received(8)
        gathered[:, rows(right_2, 0, eighth)] += part_hl[...]
        start(10)
        received(9)
        gathered[:, rows(left_2, eighth, eighth)] += part_hr[...]
        start(11)

    def planes():
        received(10, 11)
        mine[...] = (gathered[:, rows(p2)] + part_l[...]) + part_r[...]
        start(12)

    def collect():
        received(12)
        final[:, rows(p2)] = (mine[...] + from_z[...]) * (1.0 / total)
        start(13, 14)

    def collect_on():
        received(13)
        start(15)
        received(14)
        start(16)

    def invert():
        received(15, 16)
        sent(13, 14, 15, 16)
        diagonal = lax.broadcasted_iota(jnp.int32, (BLK, BLK), 0) == lax.broadcasted_iota(
            jnp.int32, (BLK, BLK), 1
        )
        for j in range(GROUP):
            block = final[j]
            on_diagonal = jnp.where(diagonal, block, 0.0)
            trace = jnp.sum(jnp.sum(on_diagonal, axis=0, keepdims=True), axis=1, keepdims=True)
            final[j] = block + jnp.where(diagonal, trace * (0.1 / BLK), 0.0)
        sweep_inverse(final)
        result[own] = -final[...]
        start(17, 18, 21)

    def spread():
        received(17)
        start(19, 22)
        received(18)
        start(20, 23)

    def finish():
        received(19, 20)
        start(24)
        received(21, 22, 23, 24)

    def settle():
        sent(*range(13), *range(17, COPIES))

    return [
        exchange, ring1_first, ring1_second, ring2_first, ring2_second, planes, collect, collect_on,
        invert, spread, finish, settle,
    ]


def pipeline_kernel(
    total, tokens, cotangent, norm_gain, norm_bias, shard, out, grams, weight, stage, entering, arriving,
    hidden, normed, rstd, slope, gradient, leaving, returning,
    pair_send, pair_recv, z_send, z_recv, ring_send, ring_recv, twin_send, twin_recv,
    next_send, next_recv, prev_send, prev_recv, factor_send, factor_recv, *buffers,
):
    me = lax.axis_index("dp")
    section = lax.axis_index("pipe")
    core = lax.rem(me, 2)
    x = lax.rem(me // 2, 4)
    z = lax.rem(me // 8, 2)
    y = me // 16
    p1 = x + core * (y - x)
    p2 = y + core * (x - y)
    stride1 = 2 + 14 * core
    stride2 = 16 - 14 * core
    right1 = me + (wrap4(p1 + 1) - p1) * stride1
    left1 = me + (wrap4(p1 - 1) - p1) * stride1
    right2 = me + (wrap4(p2 + 1) - p2) * stride2
    left2 = me + (wrap4(p2 - 1) - p2) * stride2
    across = me + (1 - 2 * z) * 8
    sibling = me + 1 - 2 * core
    following = wrap4(section + 1)
    previous = wrap4(section - 1)
    micros, mrows, width = entering.shape
    depth = stage.shape[0]
    side = width // 2
    last = section == 3

    def remote(src, dst, send, recv, **device):
        return pltpu.make_async_remote_copy(
            src_ref=src, dst_ref=dst, send_sem=send, recv_sem=recv,
            device_id=device, device_id_type=pl.DeviceIdType.MESH,
        )

    barrier = pltpu.get_barrier_semaphore()
    for device in (sibling, right1, left1, right2, left2, across):
        pl.semaphore_signal(
            barrier, inc=1, device_id={"dp": device}, device_id_type=pl.DeviceIdType.MESH
        )
    for device in (following, previous):
        pl.semaphore_signal(
            barrier, inc=1, device_id={"pipe": device}, device_id_type=pl.DeviceIdType.MESH
        )
    pl.semaphore_wait(barrier, 8)

    mine = pl.ds(pl.multiple_of(core * (depth // 2), 8), depth // 2)
    theirs = pl.ds(pl.multiple_of((1 - core) * (depth // 2), 8), depth // 2)
    pair = remote(shard.at[1 - core], stage.at[mine], pair_send, pair_recv, dp=sibling)
    pair.start()
    stage[mine] = shard[core]
    remote(stage.at[theirs], stage.at[theirs], pair_send, pair_recv, dp=sibling).wait_recv()

    def block(part, a, b, plane, columns=None):
        chip = (a + part * (b - a)) + 4 * plane + 8 * (b + part * (a - b))
        rows = pl.ds(pl.multiple_of(chip * depth, 16), depth)
        if columns is None:
            return weight.at[part, rows]
        return weight.at[part, rows, columns]

    chip = me // 2
    weight[core, pl.ds(pl.multiple_of(chip * depth, 16), depth)] = stage[...].astype(jnp.bfloat16)

    started = []

    def send(slot, ref, device):
        item = remote(ref, ref, ring_send.at[slot], ring_recv.at[slot], dp=device)
        item.start()
        started.append(item)

    def await_block(slot, ref, device):
        remote(ref, ref, ring_send.at[slot], ring_recv.at[slot], dp=device).wait_recv()

    twins = []

    def mirror(slot, a, b, plane):
        ref = block(core, a, b, plane)
        item = remote(ref, ref, twin_send.at[slot], twin_recv.at[slot], dp=sibling)
        item.start()
        twins.append(item)

    own = block(core, p1, p2, z)
    z_copy = remote(own, own, z_send, z_recv, dp=across)
    z_copy.start()

    low, high = pl.ds(0, side // 2), pl.ds(side // 2, side // 2)
    a_order = [p1, wrap4(p1 - 1), wrap4(p1 + 1), wrap4(p1 + 2)]
    b_order = [p2, wrap4(p2 - 1), wrap4(p2 + 1), wrap4(p2 + 2)]
    for turn in range(2):
        plane = z if turn == 0 else 1 - z
        base = 20 * turn
        if turn == 1:
            got = block(core, p1, p2, plane)
            remote(got, got, z_send, z_recv, dp=across).wait_recv()

        def line(i, j, columns=None):
            return block(core, a_order[i], b_order[j], plane, columns)

        def second_start(i):
            send(base + 4 + 4 * i, line(i, 0), right2)
            send(base + 5 + 4 * i, line(i, 0), left2)
            mirror(16 * turn + 4 * i, a_order[i], b_order[0], plane)

        def second_pass(i):
            await_block(base + 4 + 4 * i, line(i, 1), left2)
            send(base + 6 + 4 * i, line(i, 1, low), right2)
            mirror(16 * turn + 4 * i + 1, a_order[i], b_order[1], plane)
            await_block(base + 5 + 4 * i, line(i, 2), right2)
            send(base + 7 + 4 * i, line(i, 2, high), left2)
            mirror(16 * turn + 4 * i + 2, a_order[i], b_order[2], plane)

        def second_end(i):
            await_block(base + 6 + 4 * i, line(i, 3, low), left2)
            await_block(base + 7 + 4 * i, line(i, 3, high), right2)
            mirror(16 * turn + 4 * i + 3, a_order[i], b_order[3], plane)

        send(base, line(0, 0), right1)
        send(base + 1, line(0, 0), left1)
        second_start(0)
        await_block(base, line(1, 0), left1)
        send(base + 2, line(1, 0, low), right1)
        second_start(1)
        await_block(base + 1, line(2, 0), right1)
        send(base + 3, line(2, 0, high), left1)
        second_start(2)
        second_pass(0)
        await_block(base + 2, line(3, 0, low), left1)
        await_block(base + 3, line(3, 0, high), right1)
        second_start(3)
        second_pass(1)
        second_end(0)
        second_pass(2)
        second_end(1)
        second_pass(3)
        second_end(2)
        second_end(3)

    for turn in range(2):
        plane = z if turn == 0 else 1 - z
        for i in range(4):
            for j in range(4):
                ref = block(1 - core, b_order[i], a_order[j], plane)
                slot = 16 * turn + 4 * i + j
                remote(ref, ref, twin_send.at[slot], twin_recv.at[slot], dp=sibling).wait_recv()

    gain = norm_gain[...]
    bias = norm_bias[...]
    tiles = width // TILE

    def half_tile(t):
        half = tiles // 2
        return t // half, slice(t % half * TILE, (t % half + 1) * TILE)

    def onward(m, piece):
        cols = pl.ds(piece * (width // PIECES), width // PIECES)
        return remote(
            leaving.at[m, :, cols], entering.at[m, :, cols], next_send.at[m, piece],
            next_recv.at[m, piece], pipe=following,
        )

    def forward(m, carry):
        @pl.when(section == 0)
        def _():
            entering[m] = tokens[m]

        @pl.when(section > 0)
        def _():
            for piece in range(PIECES):
                onward(m, piece).wait_recv()

        xf = entering[m].astype(F32)
        mean = jnp.mean(xf, axis=-1, keepdims=True)
        centered = xf - mean
        var = jnp.mean(centered * centered, axis=-1, keepdims=True)
        scale = lax.rsqrt(var + 1e-05)
        unit = centered * scale
        normed[m] = unit
        rstd[m] = jnp.broadcast_to(scale, rstd.shape[1:])
        hidden[m] = (unit * gain + bias).astype(jnp.bfloat16)

        for piece in range(PIECES):
            for t in range(piece * tiles // PIECES, (piece + 1) * tiles // PIECES):
                part, inside = half_tile(t)
                cols = slice(t * TILE, (t + 1) * TILE)
                u = jnp.dot(hidden[m], weight[part, :, inside], preferred_element_type=F32)
                square = u * u
                bent = jnp.tanh(SLOPE * (u * (1.0 + CUBIC * square)))
                half = 0.5 * (1.0 + bent)
                slope[m, :, cols] = half + (0.5 * SLOPE) * u * (1.0 - bent * bent) * (
                    1.0 + (3.0 * CUBIC) * square
                )
                leaving[m, :, cols] = (entering[m, :, cols].astype(F32) + u * half).astype(
                    jnp.bfloat16
                )

            @pl.when(section < 3)
            def _():
                onward(m, piece).start()

        return carry

    lax.fori_loop(0, micros, forward, 0)

    def gram(which, rows):
        blocks = width // BLK
        for j in range(2 * 4 * GROUP):
            at = (which, j // (4 * GROUP), j // GROUP % 4, j % GROUP)
            if j >= blocks:
                grams[at] = jnp.eye(BLK, dtype=F32)
                continue
            piece = rows[:, :, j * BLK : (j + 1) * BLK].reshape(micros * mrows, BLK)
            grams[at] = lax.dot_general(
                piece, piece, (((0,), (0,)), ((), ())), preferred_element_type=F32
            )

    place = (core, p1, p2, sibling, right1, left1, right2, left2, across)
    a_stages, g_stages = (
        factor_stages(which, place, remote, total, grams, out, buffers, factor_send, factor_recv)
        for which in range(2)
    )

    def run(stages, condition):
        @pl.when(condition)
        def _():
            for stage_ in stages:
                stage_()

    gram(0, hidden)
    run(a_stages[:1], section >= 0)
    run(a_stages[1:8], section < 3)
    run(a_stages[8:11], section < 2)

    def backward(m, carry):
        @pl.when(last)
        def _():
            arriving[m] = cotangent[m]

        @pl.when(section < 3)
        def _():
            ref = arriving.at[m]
            remote(ref, ref, prev_send.at[m], prev_recv.at[m], pipe=following).wait_recv()

        gradient[m] = (slope[m] * arriving[m].astype(F32)).astype(jnp.bfloat16)

        @pl.when(section > 0)
        def _():
            for t in range(tiles):
                rows = slice(t * TILE, (t + 1) * TILE)
                back = sum(
                    lax.dot_general(
                        gradient[m, :, part * side : (part + 1) * side], weight[part, rows, :],
                        (((1,), (1,)), ((), ())), preferred_element_type=F32,
                    )
                    for part in range(2)
                )
                slope[m, :, rows] = back * norm_gain[:, rows]

            back = slope[m]
            unit = normed[m]
            along = jnp.mean(back * unit, axis=-1, keepdims=True)
            level = jnp.mean(back, axis=-1, keepdims=True)
            change = rstd[m, :, :1] * (back - level - unit * along)
            returning[m] = (arriving[m].astype(F32) + change).astype(jnp.bfloat16)
            remote(
                returning.at[m], arriving.at[m], prev_send.at[m], prev_recv.at[m], pipe=previous
            ).start()

        for stage_index in range(1, 4):
            run(a_stages[stage_index : stage_index + 1], last & (m == stage_index - 1))
        return carry

    lax.fori_loop(0, micros, backward, 0)

    run(a_stages[4:8], last)
    gram(1, gradient)
    g_stages[0]()
    run(a_stages[8:11], section >= 2)
    for stage_ in g_stages[1:]:
        stage_()
    a_stages[11]()

    pair.wait_send()
    z_copy.wait_send()
    for item in started + twins:
        item.wait_send()

    def drain(m, carry):
        @pl.when(section < 3)
        def _():
            for piece in range(PIECES):
                onward(m, piece).wait_send()

        @pl.when(section > 0)
        def _():
            remote(
                returning.at[m], arriving.at[m], prev_send.at[m], prev_recv.at[m], pipe=previous
            ).wait_send()

        return carry

    lax.fori_loop(0, micros, drain, 0)


def per_device(tokens, cotangent, norm_gain, norm_bias, proj_weight):
    rows, width = tokens.shape
    depth = 2 * proj_weight.shape[1]
    mrows = rows // MICRO
    blocks = width // BLK
    shard = proj_weight[0].astype(F32).reshape(depth // 2, 2, width // 2).swapaxes(0, 1)
    by_micro = (MICRO, mrows, width)
    every = (2, 4, GROUP, BLK, BLK)
    vmem = pl.BlockSpec(memory_space=pltpu.VMEM)
    dma = pltpu.SemaphoreType.DMA

    def pair_of(*shape):
        return pltpu.VMEM((2,) + shape, F32)

    inverses = pl.pallas_call(
        functools.partial(pipeline_kernel, float(rows * lax.axis_size("dp"))),
        out_shape=jax.ShapeDtypeStruct((2,) + every, F32),
        in_specs=[vmem] * 5,
        out_specs=vmem,
        scratch_shapes=[
            pair_of(*every),
            pltpu.VMEM((2, width, width // 2), jnp.bfloat16),
            pltpu.VMEM((depth, width // 2), F32),
            pltpu.VMEM(by_micro, jnp.bfloat16),
            pltpu.VMEM(by_micro, jnp.bfloat16),
            pltpu.VMEM(by_micro, jnp.bfloat16),
            pltpu.VMEM(by_micro, F32),
            pltpu.VMEM((MICRO, mrows, BLK), F32),
            pltpu.VMEM(by_micro, F32),
            pltpu.VMEM(by_micro, jnp.bfloat16),
            pltpu.VMEM(by_micro, jnp.bfloat16),
            pltpu.VMEM(by_micro, jnp.bfloat16),
            dma, dma, dma, dma, dma((40,)), dma((40,)), dma((32,)), dma((32,)),
            dma((MICRO, PIECES)), dma((MICRO, PIECES)), dma((MICRO,)), dma((MICRO,)),
            dma((2, COPIES)), dma((2, COPIES)),
            pair_of(4, GROUP, BLK, BLK),
            pair_of(4, GROUP, BLK, BLK),
            pair_of(GROUP, BLK // 2, BLK),
            pair_of(GROUP, BLK // 2, BLK),
            pair_of(GROUP, BLK, BLK),
            pair_of(GROUP, BLK, BLK),
            pair_of(GROUP, BLK // 8, BLK),
            pair_of(GROUP, BLK // 8, BLK),
            pair_of(GROUP, BLK // 4, BLK),
            pair_of(GROUP, BLK // 4, BLK),
            pair_of(GROUP, BLK // 4, BLK),
            pair_of(GROUP, BLK // 4, BLK),
            pair_of(GROUP, BLK, BLK),
            pair_of(GROUP, BLK, BLK),
        ],
        compiler_params=pltpu.CompilerParams(
            collective_id=0, has_side_effects=True, vmem_limit_bytes=56 * 1024 * 1024
        ),
    )(tokens.reshape(by_micro), cotangent.reshape(by_micro), norm_gain, norm_bias, shard)
    inverses = inverses.reshape(2, 8 * GROUP, BLK, BLK)[:, :blocks]
    return (inverses[:1], inverses[1:])


def solution(mesh):
    in_specs = (
        P("dp", None),
        P("dp", None),
        P("pipe", None),
        P("pipe", None),
        P("pipe", "dp", None),
    )
    out_specs = (P("pipe", None, None, None), P("pipe", None, None, None))
    return jax.shard_map(
        per_device, mesh=mesh, in_specs=in_specs, out_specs=out_specs, check_vma=False
    )
```

```python
import functools
import jax
import jax.numpy as jnp
from jax import lax
from jax.experimental import pallas as pl
from jax.experimental.pallas import tpu as pltpu
from jax.sharding import PartitionSpec as P

BLK = 128
PANEL = 16
TILE = 256
MICRO = 4
PIECES = 2
GROUP = 3
COPIES = 21
SLOPE = (2.0 / 3.141592653589793) ** 0.5
CUBIC = 0.044715
F32 = jnp.float32


def wrap4(value):
    return lax.rem(value + 4, 4)


def three_parts(value):
    high = value.astype(jnp.bfloat16)
    rest = value - high.astype(F32)
    middle = rest.astype(jnp.bfloat16)
    low = (rest - middle.astype(F32)).astype(jnp.bfloat16)
    return high, middle, low


def outer_sum(left, right):
    lh, lm, ll = three_parts(left)
    rh, rm, rl = three_parts(right)
    lhs = jnp.concatenate([lh, lh, lm, lh, ll, lm], axis=0)
    rhs = jnp.concatenate([rh, rm, rh, rl, rh, rm], axis=0)
    return lax.dot_general(lhs, rhs, (((0,), (0,)), ((), ())), preferred_element_type=F32)


def sweep_inverse(m_ref):
    count = m_ref.shape[0]
    lane = lax.broadcasted_iota(jnp.int32, (PANEL, BLK), 1)
    row = lax.broadcasted_iota(jnp.int32, (PANEL, BLK), 0)
    lane_full = lax.broadcasted_iota(jnp.int32, (BLK, BLK), 1)
    for base in range(0, BLK, PANEL):
        in_block = lane // PANEL == base // PANEL
        in_block_full = lane_full // PANEL == base // PANEL
        select = jnp.where(lane == base + row, 1.0, 0.0).astype(F32)
        rows = [m_ref[j, base : base + PANEL, :] for j in range(count)]
        work = list(rows)
        columns = [
            [jnp.broadcast_to(panel[:, base + i : base + i + 1], panel.shape) for i in range(PANEL)]
            for panel in rows
        ]
        for i in range(PANEL):
            for j in range(count):
                panel, column = work[j], columns[j]
                inv = 1.0 / column[i][i : i + 1]
                for k in range(i + 1, PANEL):
                    pivot_row = column[k][i : i + 1] * inv
                    column[k] = jnp.where(row == i, pivot_row, column[k] - column[i] * pivot_row)
                scaled = jnp.where(lane[:1] == base + i, inv, panel[i : i + 1] * inv)
                rest = jnp.where(lane == base + i, 0.0, panel) - column[i] * scaled
                work[j] = jnp.where(row == i, scaled, rest)
        for j in range(count):
            solved = work[j]
            outside = jnp.where(in_block, 0.0, solved)
            left = jnp.concatenate([jnp.where(in_block, 0.0, rows[j]), outside], axis=0)
            right = jnp.concatenate([-outside, select], axis=0)
            update = outer_sum(left, right)
            m_ref[j] = jnp.where(in_block_full, 0.0, m_ref[j]) + update
            m_ref[j, base : base + PANEL, :] = outside - jnp.where(in_block, solved, 0.0)


def factor_stages(which, place, remote, total, grams, out, buffers, send_sem, recv_sem):
    core, p1, p2, sibling, ring1, ring2, across = place
    from_core, summed, ring1_in, ring2_in, mine, from_z, gathered, final = (
        buffer.at[which] for buffer in buffers
    )
    other = 1 - core
    ours = [wrap4(p1 + d) for d in range(4)]
    theirs = [wrap4(p2 + d) for d in range(4)]
    order = (2, 1, 3, 0)
    quarter = BLK // 4

    def rows(part):
        return pl.ds(pl.multiple_of(part * quarter, quarter), quarter)

    result = out.at[which, core]
    table = {}
    for d in range(4):
        table[d] = (
            grams.at[which, other, theirs[d]], from_core.at[theirs[d]], sibling, from_core.at[ours[d]]
        )
        table[16 + d] = (
            result.at[ours[d]], result.at[ours[d]], sibling, out.at[which, other, theirs[d]]
        )
    for d in range(1, 4):
        table[3 + d] = (summed.at[ours[d]], ring1_in.at[d - 1], ring1[d], ring1_in.at[d - 1])
        table[6 + d] = (gathered.at[:, rows(theirs[d])], ring2_in.at[d - 1], ring2[d], ring2_in.at[d - 1])
        table[9 + d] = (
            final.at[:, rows(p2)], final.at[:, rows(p2)], ring2[d], final.at[:, rows(theirs[4 - d])]
        )
        table[12 + d] = (result.at[p1], result.at[p1], ring1[d], result.at[ours[4 - d]])
    table[20] = (mine, from_z, across, from_z)

    def start(*indices):
        for k in indices:
            src, dst, device, _ = table[k]
            remote(src, dst, send_sem.at[which, k], recv_sem.at[which, k], dp=device).start()

    def received(*indices):
        for k in indices:
            _, _, device, landed = table[k]
            remote(landed, landed, send_sem.at[which, k], recv_sem.at[which, k], dp=device).wait_recv()

    def sent(*indices):
        for k in indices:
            src, dst, device, _ = table[k]
            remote(src, dst, send_sem.at[which, k], recv_sem.at[which, k], dp=device).wait_send()

    def exchange():
        start(*order)

    def over_ring1():
        for d in order:
            received(d)
            summed[ours[d]] = grams[which, core, ours[d]] + from_core[ours[d]]
            if d:
                start(3 + d)

    def over_ring2():
        received(4, 5, 6)
        gathered[...] = (summed[p1] + ring1_in[0]) + (ring1_in[1] + ring1_in[2])
        start(8, 7, 9)

    def over_planes():
        received(7, 8, 9)
        mine[...] = (gathered[:, rows(p2)] + ring2_in[0]) + (ring2_in[1] + ring2_in[2])
        start(20)

    def collect():
        received(20)
        final[:, rows(p2)] = (mine[...] + from_z[...]) * (1.0 / total)
        start(11, 10, 12)

    def invert():
        received(10, 11, 12)
        sent(10, 11, 12)
        diagonal = lax.broadcasted_iota(jnp.int32, (BLK, BLK), 0) == lax.broadcasted_iota(
            jnp.int32, (BLK, BLK), 1
        )
        for j in range(GROUP):
            block = final[j]
            on_diagonal = jnp.where(diagonal, block, 0.0)
            trace = jnp.sum(jnp.sum(on_diagonal, axis=0, keepdims=True), axis=1, keepdims=True)
            final[j] = block + jnp.where(diagonal, trace * (0.1 / BLK), 0.0)
        sweep_inverse(final)
        result[p1] = -final[...]
        start(14, 13, 15, 16)

    def spread():
        for d in (1, 3, 2):
            received(12 + 4 - d)
            start(16 + d)

    def finish():
        received(16, 17, 18, 19)

    def settle():
        sent(*range(10), *range(13, COPIES))

    return [exchange, over_ring1, over_ring2, over_planes, collect, invert, spread, finish, settle]


def pipeline_kernel(
    total, tokens, cotangent, norm_gain, norm_bias, shard, out, grams, weight, stage, entering, arriving,
    hidden, normed, rstd, slope, gradient, leaving, returning,
    pair_send, pair_recv, z_send, z_recv, ring_send, ring_recv, twin_send, twin_recv,
    next_send, next_recv, prev_send, prev_recv, factor_send, factor_recv, *buffers,
):
    me = lax.axis_index("dp")
    section = lax.axis_index("pipe")
    core = lax.rem(me, 2)
    x = lax.rem(me // 2, 4)
    z = lax.rem(me // 8, 2)
    y = me // 16
    p1 = x + core * (y - x)
    p2 = y + core * (x - y)
    stride1 = 2 + 14 * core
    stride2 = 16 - 14 * core
    right1 = me + (wrap4(p1 + 1) - p1) * stride1
    left1 = me + (wrap4(p1 - 1) - p1) * stride1
    right2 = me + (wrap4(p2 + 1) - p2) * stride2
    left2 = me + (wrap4(p2 - 1) - p2) * stride2
    across = me + (1 - 2 * z) * 8
    sibling = me + 1 - 2 * core
    following = wrap4(section + 1)
    previous = wrap4(section - 1)
    micros, mrows, width = entering.shape
    depth = stage.shape[0]
    side = width // 2
    last = section == 3

    def remote(src, dst, send, recv, **device):
        return pltpu.make_async_remote_copy(
            src_ref=src, dst_ref=dst, send_sem=send, recv_sem=recv,
            device_id=device, device_id_type=pl.DeviceIdType.MESH,
        )

    barrier = pltpu.get_barrier_semaphore()
    opposite1 = me + (wrap4(p1 + 2) - p1) * stride1
    opposite2 = me + (wrap4(p2 + 2) - p2) * stride2
    for device in (sibling, right1, left1, opposite1, right2, left2, opposite2, across):
        pl.semaphore_signal(
            barrier, inc=1, device_id={"dp": device}, device_id_type=pl.DeviceIdType.MESH
        )
    for device in (following, previous):
        pl.semaphore_signal(
            barrier, inc=1, device_id={"pipe": device}, device_id_type=pl.DeviceIdType.MESH
        )
    pl.semaphore_wait(barrier, 10)

    mine = pl.ds(pl.multiple_of(core * (depth // 2), 8), depth // 2)
    theirs = pl.ds(pl.multiple_of((1 - core) * (depth // 2), 8), depth // 2)
    pair = remote(shard.at[1 - core], stage.at[mine], pair_send, pair_recv, dp=sibling)
    pair.start()
    stage[mine] = shard[core]
    remote(stage.at[theirs], stage.at[theirs], pair_send, pair_recv, dp=sibling).wait_recv()

    def block(part, a, b, plane, columns=None):
        chip = (a + part * (b - a)) + 4 * plane + 8 * (b + part * (a - b))
        rows = pl.ds(pl.multiple_of(chip * depth, 16), depth)
        if columns is None:
            return weight.at[part, rows]
        return weight.at[part, rows, columns]

    chip = me // 2
    weight[core, pl.ds(pl.multiple_of(chip * depth, 16), depth)] = stage[...].astype(jnp.bfloat16)

    started = []

    def send(slot, ref, device):
        item = remote(ref, ref, ring_send.at[slot], ring_recv.at[slot], dp=device)
        item.start()
        started.append(item)

    def await_block(slot, ref, device):
        remote(ref, ref, ring_send.at[slot], ring_recv.at[slot], dp=device).wait_recv()

    twins = []

    def mirror(slot, a, b, plane):
        ref = block(core, a, b, plane)
        item = remote(ref, ref, twin_send.at[slot], twin_recv.at[slot], dp=sibling)
        item.start()
        twins.append(item)

    own = block(core, p1, p2, z)
    z_copy = remote(own, own, z_send, z_recv, dp=across)
    z_copy.start()

    low, high = pl.ds(0, side // 2), pl.ds(side // 2, side // 2)
    a_order = [p1, wrap4(p1 - 1), wrap4(p1 + 1), wrap4(p1 + 2)]
    b_order = [p2, wrap4(p2 - 1), wrap4(p2 + 1), wrap4(p2 + 2)]
    def gather_steps(turn):
        plane = z if turn == 0 else 1 - z
        base = 20 * turn

        def line(i, j, columns=None):
            return block(core, a_order[i], b_order[j], plane, columns)

        def second_start(i):
            send(base + 4 + 4 * i, line(i, 0), right2)
            send(base + 5 + 4 * i, line(i, 0), left2)
            mirror(16 * turn + 4 * i, a_order[i], b_order[0], plane)

        def second_pass(i):
            await_block(base + 4 + 4 * i, line(i, 1), left2)
            send(base + 6 + 4 * i, line(i, 1, low), right2)
            mirror(16 * turn + 4 * i + 1, a_order[i], b_order[1], plane)
            await_block(base + 5 + 4 * i, line(i, 2), right2)
            send(base + 7 + 4 * i, line(i, 2, high), left2)
            mirror(16 * turn + 4 * i + 2, a_order[i], b_order[2], plane)

        def second_end(i):
            await_block(base + 6 + 4 * i, line(i, 3, low), left2)
            await_block(base + 7 + 4 * i, line(i, 3, high), right2)
            mirror(16 * turn + 4 * i + 3, a_order[i], b_order[3], plane)

        def enter():
            if turn == 1:
                got = block(core, p1, p2, plane)
                remote(got, got, z_send, z_recv, dp=across).wait_recv()
            send(base, line(0, 0), right1)
            send(base + 1, line(0, 0), left1)
            second_start(0)

        def from_left():
            await_block(base, line(1, 0), left1)
            send(base + 2, line(1, 0, low), right1)
            second_start(1)

        def from_right():
            await_block(base + 1, line(2, 0), right1)
            send(base + 3, line(2, 0, high), left1)
            second_start(2)

        def from_opposite():
            await_block(base + 2, line(3, 0, low), left1)
            await_block(base + 3, line(3, 0, high), right1)
            second_start(3)

        return [
            enter, from_left, from_right, lambda: second_pass(0), from_opposite,
            lambda: second_pass(1), lambda: second_end(0), lambda: second_pass(2),
            lambda: second_end(1), lambda: second_pass(3), lambda: second_end(2),
            lambda: second_end(3),
        ]

    near, far = gather_steps(0), gather_steps(1)
    for step in (
        near[:7] + far[:1] + near[7:9] + far[1:2] + near[9:10] + far[2:3] + near[10:11]
        + far[3:4] + near[11:] + far[4:]
    ):
        step()

    for turn in range(2):
        plane = z if turn == 0 else 1 - z
        for i in range(4):
            for j in range(4):
                ref = block(1 - core, b_order[i], a_order[j], plane)
                slot = 16 * turn + 4 * i + j
                remote(ref, ref, twin_send.at[slot], twin_recv.at[slot], dp=sibling).wait_recv()

    gain = norm_gain[...]
    bias = norm_bias[...]
    tiles = width // TILE

    def half_tile(t):
        half = tiles // 2
        return t // half, slice(t % half * TILE, (t % half + 1) * TILE)

    def onward(m, piece):
        cols = pl.ds(piece * (width // PIECES), width // PIECES)
        return remote(
            leaving.at[m, :, cols], entering.at[m, :, cols], next_send.at[m, piece],
            next_recv.at[m, piece], pipe=following,
        )

    def forward(m, carry):
        @pl.when(section == 0)
        def _():
            entering[m] = tokens[m]

        @pl.when(section > 0)
        def _():
            for piece in range(PIECES):
                onward(m, piece).wait_recv()

        xf = entering[m].astype(F32)
        mean = jnp.mean(xf, axis=-1, keepdims=True)
        centered = xf - mean
        var = jnp.mean(centered * centered, axis=-1, keepdims=True)
        scale = lax.rsqrt(var + 1e-05)
        unit = centered * scale
        normed[m] = unit
        rstd[m] = jnp.broadcast_to(scale, rstd.shape[1:])
        hidden[m] = (unit * gain + bias).astype(jnp.bfloat16)

        for piece in range(PIECES):
            for t in range(piece * tiles // PIECES, (piece + 1) * tiles // PIECES):
                part, inside = half_tile(t)
                cols = slice(t * TILE, (t + 1) * TILE)
                u = jnp.dot(hidden[m], weight[part, :, inside], preferred_element_type=F32)
                square = u * u
                bent = jnp.tanh(SLOPE * (u * (1.0 + CUBIC * square)))
                half = 0.5 * (1.0 + bent)
                slope[m, :, cols] = half + (0.5 * SLOPE) * u * (1.0 - bent * bent) * (
                    1.0 + (3.0 * CUBIC) * square
                )
                leaving[m, :, cols] = (entering[m, :, cols].astype(F32) + u * half).astype(
                    jnp.bfloat16
                )

            @pl.when(section < 3)
            def _():
                onward(m, piece).start()

        return carry

    lax.fori_loop(0, micros, forward, 0)

    def gram(which, rows):
        blocks = width // BLK
        for j in range(2 * 4 * GROUP):
            at = (which, j // (4 * GROUP), j // GROUP % 4, j % GROUP)
            if j >= blocks:
                grams[at] = jnp.eye(BLK, dtype=F32)
                continue
            piece = rows[:, :, j * BLK : (j + 1) * BLK].reshape(micros * mrows, BLK)
            grams[at] = lax.dot_general(
                piece, piece, (((0,), (0,)), ((), ())), preferred_element_type=F32
            )

    ring1 = [me + (wrap4(p1 + d) - p1) * stride1 for d in range(4)]
    ring2 = [me + (wrap4(p2 + d) - p2) * stride2 for d in range(4)]
    place = (core, p1, p2, sibling, ring1, ring2, across)
    a_stages, g_stages = (
        factor_stages(which, place, remote, total, grams, out, buffers, factor_send, factor_recv)
        for which in range(2)
    )

    def run(stages, condition):
        @pl.when(condition)
        def _():
            for stage_ in stages:
                stage_()

    @pl.when(section < 3)
    def _():
        gram(0, hidden)

    run(a_stages[:3], section < 3)
    run(a_stages[3:8], section < 2)

    def backward(m, carry):
        @pl.when(last)
        def _():
            arriving[m] = cotangent[m]

        @pl.when(section < 3)
        def _():
            ref = arriving.at[m]
            remote(ref, ref, prev_send.at[m], prev_recv.at[m], pipe=following).wait_recv()

        gradient[m] = (slope[m] * arriving[m].astype(F32)).astype(jnp.bfloat16)

        @pl.when(section > 0)
        def _():
            for t in range(tiles):
                rows = slice(t * TILE, (t + 1) * TILE)
                back = sum(
                    lax.dot_general(
                        gradient[m, :, part * side : (part + 1) * side], weight[part, rows, :],
                        (((1,), (1,)), ((), ())), preferred_element_type=F32,
                    )
                    for part in range(2)
                )
                slope[m, :, rows] = back * norm_gain[:, rows]

            back = slope[m]
            unit = normed[m]
            along = jnp.mean(back * unit, axis=-1, keepdims=True)
            level = jnp.mean(back, axis=-1, keepdims=True)
            change = rstd[m, :, :1] * (back - level - unit * along)
            returning[m] = (arriving[m].astype(F32) + change).astype(jnp.bfloat16)
            remote(
                returning.at[m], arriving.at[m], prev_send.at[m], prev_recv.at[m], pipe=previous
            ).start()

        return carry

    lax.fori_loop(0, micros, backward, 0)

    gram(1, gradient)
    g_stages[0]()

    @pl.when(last)
    def _():
        gram(0, hidden)

    for k in range(8):
        run(a_stages[k : k + 1], last if k < 3 else section >= 2)
        if k:
            g_stages[k]()
    a_stages[8]()
    g_stages[8]()

    pair.wait_send()
    z_copy.wait_send()
    for item in started + twins:
        item.wait_send()

    def drain(m, carry):
        @pl.when(section < 3)
        def _():
            for piece in range(PIECES):
                onward(m, piece).wait_send()

        @pl.when(section > 0)
        def _():
            remote(
                returning.at[m], arriving.at[m], prev_send.at[m], prev_recv.at[m], pipe=previous
            ).wait_send()

        return carry

    lax.fori_loop(0, micros, drain, 0)


def per_device(tokens, cotangent, norm_gain, norm_bias, proj_weight):
    rows, width = tokens.shape
    depth = 2 * proj_weight.shape[1]
    mrows = rows // MICRO
    blocks = width // BLK
    shard = proj_weight[0].astype(F32).reshape(depth // 2, 2, width // 2).swapaxes(0, 1)
    by_micro = (MICRO, mrows, width)
    every = (2, 4, GROUP, BLK, BLK)
    vmem = pl.BlockSpec(memory_space=pltpu.VMEM)
    dma = pltpu.SemaphoreType.DMA

    def pair_of(*shape):
        return pltpu.VMEM((2,) + shape, F32)

    inverses = pl.pallas_call(
        functools.partial(pipeline_kernel, float(rows * lax.axis_size("dp"))),
        out_shape=jax.ShapeDtypeStruct((2,) + every, F32),
        in_specs=[vmem] * 5,
        out_specs=vmem,
        scratch_shapes=[
            pair_of(*every),
            pltpu.VMEM((2, width, width // 2), jnp.bfloat16),
            pltpu.VMEM((depth, width // 2), F32),
            pltpu.VMEM(by_micro, jnp.bfloat16),
            pltpu.VMEM(by_micro, jnp.bfloat16),
            pltpu.VMEM(by_micro, jnp.bfloat16),
            pltpu.VMEM(by_micro, F32),
            pltpu.VMEM((MICRO, mrows, BLK), F32),
            pltpu.VMEM(by_micro, F32),
            pltpu.VMEM(by_micro, jnp.bfloat16),
            pltpu.VMEM(by_micro, jnp.bfloat16),
            pltpu.VMEM(by_micro, jnp.bfloat16),
            dma, dma, dma, dma, dma((40,)), dma((40,)), dma((32,)), dma((32,)),
            dma((MICRO, PIECES)), dma((MICRO, PIECES)), dma((MICRO,)), dma((MICRO,)),
            dma((2, COPIES)), dma((2, COPIES)),
            pair_of(4, GROUP, BLK, BLK),
            pair_of(4, GROUP, BLK, BLK),
            pair_of(3, GROUP, BLK, BLK),
            pair_of(3, GROUP, BLK // 4, BLK),
            pair_of(GROUP, BLK // 4, BLK),
            pair_of(GROUP, BLK // 4, BLK),
            pair_of(GROUP, BLK, BLK),
            pair_of(GROUP, BLK, BLK),
        ],
        compiler_params=pltpu.CompilerParams(
            collective_id=0, has_side_effects=True, vmem_limit_bytes=56 * 1024 * 1024
        ),
    )(tokens.reshape(by_micro), cotangent.reshape(by_micro), norm_gain, norm_bias, shard)
    inverses = inverses.reshape(2, 8 * GROUP, BLK, BLK)[:, :blocks]
    return (inverses[:1], inverses[1:])


def solution(mesh):
    in_specs = (
        P("dp", None),
        P("dp", None),
        P("pipe", None),
        P("pipe", None),
        P("pipe", "dp", None),
    )
    out_specs = (P("pipe", None, None, None), P("pipe", None, None, None))
    return jax.shard_map(
        per_device, mesh=mesh, in_specs=in_specs, out_specs=out_specs, check_vma=False
    )
```

```python
import functools
import jax
import jax.numpy as jnp
from jax import lax
from jax.experimental import pallas as pl
from jax.experimental.pallas import tpu as pltpu
from jax.sharding import PartitionSpec as P

BLK = 128
PANEL = 16
TILE = 256
MICRO = 4
PIECES = 2
BACKS = 5
GROUP = 3
COPIES = 21
SLOPE = (2.0 / 3.141592653589793) ** 0.5
CUBIC = 0.044715
F32 = jnp.float32


def wrap4(value):
    return lax.rem(value + 4, 4)


def three_parts(value):
    high = value.astype(jnp.bfloat16)
    rest = value - high.astype(F32)
    middle = rest.astype(jnp.bfloat16)
    low = (rest - middle.astype(F32)).astype(jnp.bfloat16)
    return high, middle, low


def outer_sum(left, right):
    lh, lm, ll = three_parts(left)
    rh, rm, rl = three_parts(right)
    lhs = jnp.concatenate([lh, lh, lm, lh, ll, lm], axis=0)
    rhs = jnp.concatenate([rh, rm, rh, rl, rh, rm], axis=0)
    return lax.dot_general(lhs, rhs, (((0,), (0,)), ((), ())), preferred_element_type=F32)


def sweep_inverse(m_ref):
    count = m_ref.shape[0]
    lane = lax.broadcasted_iota(jnp.int32, (PANEL, BLK), 1)
    row = lax.broadcasted_iota(jnp.int32, (PANEL, BLK), 0)
    lane_full = lax.broadcasted_iota(jnp.int32, (BLK, BLK), 1)
    for base in range(0, BLK, PANEL):
        in_block = lane // PANEL == base // PANEL
        in_block_full = lane_full // PANEL == base // PANEL
        select = jnp.where(lane == base + row, 1.0, 0.0).astype(F32)
        rows = [m_ref[j, base : base + PANEL, :] for j in range(count)]
        work = list(rows)
        columns = [
            [jnp.broadcast_to(panel[:, base + i : base + i + 1], panel.shape) for i in range(PANEL)]
            for panel in rows
        ]
        for i in range(PANEL):
            for j in range(count):
                panel, column = work[j], columns[j]
                inv = 1.0 / column[i][i : i + 1]
                for k in range(i + 1, PANEL):
                    pivot_row = column[k][i : i + 1] * inv
                    column[k] = jnp.where(row == i, pivot_row, column[k] - column[i] * pivot_row)
                scaled = jnp.where(lane[:1] == base + i, inv, panel[i : i + 1] * inv)
                rest = jnp.where(lane == base + i, 0.0, panel) - column[i] * scaled
                work[j] = jnp.where(row == i, scaled, rest)
        for j in range(count):
            solved = work[j]
            outside = jnp.where(in_block, 0.0, solved)
            left = jnp.concatenate([jnp.where(in_block, 0.0, rows[j]), outside], axis=0)
            right = jnp.concatenate([-outside, select], axis=0)
            update = outer_sum(left, right)
            m_ref[j] = jnp.where(in_block_full, 0.0, m_ref[j]) + update
            m_ref[j, base : base + PANEL, :] = outside - jnp.where(in_block, solved, 0.0)


def factor_stages(which, place, remote, total, grams, out, buffers, send_sem, recv_sem):
    core, p1, p2, sibling, ring1, ring2, across = place
    from_core, summed, ring1_in, ring2_in, mine, from_z, gathered, final = (
        buffer.at[which] for buffer in buffers
    )
    other = 1 - core
    ours = [wrap4(p1 + d) for d in range(4)]
    theirs = [wrap4(p2 + d) for d in range(4)]
    order = (2, 1, 3, 0)
    quarter = BLK // 4

    def rows(part):
        return pl.ds(pl.multiple_of(part * quarter, quarter), quarter)

    result = out.at[which, core]
    table = {}
    for d in range(4):
        table[d] = (
            grams.at[which, other, theirs[d]], from_core.at[theirs[d]], sibling, from_core.at[ours[d]]
        )
        table[16 + d] = (
            result.at[ours[d]], result.at[ours[d]], sibling, out.at[which, other, theirs[d]]
        )
    for d in range(1, 4):
        table[3 + d] = (summed.at[ours[d]], ring1_in.at[d - 1], ring1[d], ring1_in.at[d - 1])
        table[6 + d] = (gathered.at[:, rows(theirs[d])], ring2_in.at[d - 1], ring2[d], ring2_in.at[d - 1])
        table[9 + d] = (
            final.at[:, rows(p2)], final.at[:, rows(p2)], ring2[d], final.at[:, rows(theirs[4 - d])]
        )
        table[12 + d] = (result.at[p1], result.at[p1], ring1[d], result.at[ours[4 - d]])
    table[20] = (mine, from_z, across, from_z)

    def start(*indices):
        for k in indices:
            src, dst, device, _ = table[k]
            remote(src, dst, send_sem.at[which, k], recv_sem.at[which, k], dp=device).start()

    def received(*indices):
        for k in indices:
            _, _, device, landed = table[k]
            remote(landed, landed, send_sem.at[which, k], recv_sem.at[which, k], dp=device).wait_recv()

    def sent(*indices):
        for k in indices:
            src, dst, device, _ = table[k]
            remote(src, dst, send_sem.at[which, k], recv_sem.at[which, k], dp=device).wait_send()

    def exchange():
        start(*order)

    def over_ring1():
        for d in order:
            received(d)
            summed[ours[d]] = grams[which, core, ours[d]] + from_core[ours[d]]
            if d:
                start(3 + d)

    def over_ring2():
        received(4, 5, 6)
        gathered[...] = (summed[p1] + ring1_in[0]) + (ring1_in[1] + ring1_in[2])
        start(8, 7, 9)

    def over_planes():
        received(7, 8, 9)
        mine[...] = (gathered[:, rows(p2)] + ring2_in[0]) + (ring2_in[1] + ring2_in[2])
        start(20)

    def collect():
        received(20)
        final[:, rows(p2)] = (mine[...] + from_z[...]) * (1.0 / total)
        start(11, 10, 12)

    def invert():
        received(10, 11, 12)
        sent(10, 11, 12)
        diagonal = lax.broadcasted_iota(jnp.int32, (BLK, BLK), 0) == lax.broadcasted_iota(
            jnp.int32, (BLK, BLK), 1
        )
        for j in range(GROUP):
            block = final[j]
            on_diagonal = jnp.where(diagonal, block, 0.0)
            trace = jnp.sum(jnp.sum(on_diagonal, axis=0, keepdims=True), axis=1, keepdims=True)
            final[j] = block + jnp.where(diagonal, trace * (0.1 / BLK), 0.0)
        sweep_inverse(final)
        result[p1] = -final[...]
        start(14, 13, 15, 16)

    def spread():
        for d in (1, 3, 2):
            received(12 + 4 - d)
            start(16 + d)

    def finish():
        received(16, 17, 18, 19)

    def settle():
        sent(*range(10), *range(13, COPIES))

    return [exchange, over_ring1, over_ring2, over_planes, collect, invert, spread, finish, settle]


def pipeline_kernel(
    total, tokens, cotangent, norm_gain, norm_bias, shard, out, grams, weight, stage, entering, arriving,
    hidden, normed, rstd, slope, offset, lines, gradient, leaving, returning,
    pair_send, pair_recv, z_send, z_recv, ring_send, ring_recv, twin_send, twin_recv,
    next_send, next_recv, prev_send, prev_recv, factor_send, factor_recv, *buffers,
):
    me = lax.axis_index("dp")
    section = lax.axis_index("pipe")
    core = lax.rem(me, 2)
    x = lax.rem(me // 2, 4)
    z = lax.rem(me // 8, 2)
    y = me // 16
    p1 = x + core * (y - x)
    p2 = y + core * (x - y)
    stride1 = 2 + 14 * core
    stride2 = 16 - 14 * core
    right1 = me + (wrap4(p1 + 1) - p1) * stride1
    left1 = me + (wrap4(p1 - 1) - p1) * stride1
    right2 = me + (wrap4(p2 + 1) - p2) * stride2
    left2 = me + (wrap4(p2 - 1) - p2) * stride2
    across = me + (1 - 2 * z) * 8
    sibling = me + 1 - 2 * core
    following = wrap4(section + 1)
    previous = wrap4(section - 1)
    micros, mrows, width = entering.shape
    depth = stage.shape[0]
    side = width // 2
    last = section == 3

    def remote(src, dst, send, recv, **device):
        return pltpu.make_async_remote_copy(
            src_ref=src, dst_ref=dst, send_sem=send, recv_sem=recv,
            device_id=device, device_id_type=pl.DeviceIdType.MESH,
        )

    barrier = pltpu.get_barrier_semaphore()
    opposite1 = me + (wrap4(p1 + 2) - p1) * stride1
    opposite2 = me + (wrap4(p2 + 2) - p2) * stride2
    for device in (sibling, right1, left1, opposite1, right2, left2, opposite2, across):
        pl.semaphore_signal(
            barrier, inc=1, device_id={"dp": device}, device_id_type=pl.DeviceIdType.MESH
        )
    for device in (following, previous):
        pl.semaphore_signal(
            barrier, inc=1, device_id={"pipe": device}, device_id_type=pl.DeviceIdType.MESH
        )
    pl.semaphore_wait(barrier, 10)

    mine = pl.ds(pl.multiple_of(core * (depth // 2), 8), depth // 2)
    theirs = pl.ds(pl.multiple_of((1 - core) * (depth // 2), 8), depth // 2)
    pair = remote(shard.at[1 - core], stage.at[mine], pair_send, pair_recv, dp=sibling)
    pair.start()
    stage[mine] = shard[core]
    remote(stage.at[theirs], stage.at[theirs], pair_send, pair_recv, dp=sibling).wait_recv()

    def block(part, a, b, plane, columns=None):
        chip = (a + part * (b - a)) + 4 * plane + 8 * (b + part * (a - b))
        rows = pl.ds(pl.multiple_of(chip * depth, 16), depth)
        if columns is None:
            return weight.at[part, rows]
        return weight.at[part, rows, columns]

    chip = me // 2
    weight[core, pl.ds(pl.multiple_of(chip * depth, 16), depth)] = stage[...].astype(jnp.bfloat16)

    started = []

    def send(slot, ref, device):
        item = remote(ref, ref, ring_send.at[slot], ring_recv.at[slot], dp=device)
        item.start()
        started.append(item)

    def await_block(slot, ref, device):
        remote(ref, ref, ring_send.at[slot], ring_recv.at[slot], dp=device).wait_recv()

    twins = []

    def mirror(slot, a, b, plane):
        ref = block(core, a, b, plane)
        item = remote(ref, ref, twin_send.at[slot], twin_recv.at[slot], dp=sibling)
        item.start()
        twins.append(item)

    own = block(core, p1, p2, z)
    z_copy = remote(own, own, z_send, z_recv, dp=across)
    z_copy.start()

    low, high = pl.ds(0, side // 2), pl.ds(side // 2, side // 2)
    a_order = [p1, wrap4(p1 - 1), wrap4(p1 + 1), wrap4(p1 + 2)]
    b_order = [p2, wrap4(p2 - 1), wrap4(p2 + 1), wrap4(p2 + 2)]
    def gather_steps(turn):
        plane = z if turn == 0 else 1 - z
        base = 20 * turn

        def line(i, j, columns=None):
            return block(core, a_order[i], b_order[j], plane, columns)

        def second_start(i):
            send(base + 4 + 4 * i, line(i, 0), right2)
            send(base + 5 + 4 * i, line(i, 0), left2)
            mirror(16 * turn + 4 * i, a_order[i], b_order[0], plane)

        def second_pass(i):
            await_block(base + 4 + 4 * i, line(i, 1), left2)
            send(base + 6 + 4 * i, line(i, 1, low), right2)
            mirror(16 * turn + 4 * i + 1, a_order[i], b_order[1], plane)
            await_block(base + 5 + 4 * i, line(i, 2), right2)
            send(base + 7 + 4 * i, line(i, 2, high), left2)
            mirror(16 * turn + 4 * i + 2, a_order[i], b_order[2], plane)

        def second_end(i):
            await_block(base + 6 + 4 * i, line(i, 3, low), left2)
            await_block(base + 7 + 4 * i, line(i, 3, high), right2)
            mirror(16 * turn + 4 * i + 3, a_order[i], b_order[3], plane)

        def enter():
            if turn == 1:
                got = block(core, p1, p2, plane)
                remote(got, got, z_send, z_recv, dp=across).wait_recv()
            send(base, line(0, 0), right1)
            send(base + 1, line(0, 0), left1)
            second_start(0)

        def from_left():
            await_block(base, line(1, 0), left1)
            send(base + 2, line(1, 0, low), right1)
            second_start(1)

        def from_right():
            await_block(base + 1, line(2, 0), right1)
            send(base + 3, line(2, 0, high), left1)
            second_start(2)

        def from_opposite():
            await_block(base + 2, line(3, 0, low), left1)
            await_block(base + 3, line(3, 0, high), right1)
            second_start(3)

        return [
            enter, from_left, from_right, lambda: second_pass(0), from_opposite,
            lambda: second_pass(1), lambda: second_end(0), lambda: second_pass(2),
            lambda: second_end(1), lambda: second_pass(3), lambda: second_end(2),
            lambda: second_end(3),
        ]

    near, far = gather_steps(0), gather_steps(1)
    for step in (
        near[:7] + far[:1] + near[7:9] + far[1:2] + near[9:10] + far[2:3] + near[10:11]
        + far[3:4] + near[11:] + far[4:]
    ):
        step()

    for turn in range(2):
        plane = z if turn == 0 else 1 - z
        for i in range(4):
            for j in range(4):
                ref = block(1 - core, b_order[i], a_order[j], plane)
                slot = 16 * turn + 4 * i + j
                remote(ref, ref, twin_send.at[slot], twin_recv.at[slot], dp=sibling).wait_recv()

    gain = norm_gain[...]
    bias = norm_bias[...]
    tiles = width // TILE

    def half_tile(t):
        half = tiles // 2
        return t // half, slice(t % half * TILE, (t % half + 1) * TILE)

    def onward(m, piece):
        cols = pl.ds(piece * (width // PIECES), width // PIECES)
        return remote(
            leaving.at[m, :, cols], entering.at[m, :, cols], next_send.at[m, piece],
            next_recv.at[m, piece], pipe=following,
        )

    def back(m, piece):
        cols = pl.ds(piece * (width // BACKS), width // BACKS)
        return remote(
            returning.at[m, :, cols], arriving.at[m, :, cols], prev_send.at[m, piece],
            prev_recv.at[m, piece], pipe=previous,
        )

    @pl.when(section == 0)
    def _():
        lines[...] = jnp.zeros_like(lines)

    @pl.when(section > 0)
    def _():
        row = lax.broadcasted_iota(jnp.int32, (16, width), 0)
        stack = jnp.zeros((16, width), F32)
        for k, value in enumerate(three_parts(gain) + three_parts(bias)):
            stack = jnp.where(row == k, value.astype(F32), stack)
        stack = stack.astype(jnp.bfloat16)
        for t in range(tiles):
            part, inside = half_tile(t)
            cols = slice(t * TILE, (t + 1) * TILE)
            product = jnp.dot(stack, weight[part, :, inside], preferred_element_type=F32)
            lines[0:1, cols] = product[0:1] + product[1:2] + product[2:3]
            lines[1:2, cols] = product[3:4] + product[4:5] + product[5:6]

    def forward(m, carry):
        @pl.when(section == 0)
        def _():
            entering[m] = tokens[m]

        @pl.when(section > 0)
        def _():
            for piece in range(PIECES):
                onward(m, piece).wait_recv()

        xf = entering[m].astype(F32)
        mean = jnp.mean(xf, axis=-1, keepdims=True)
        centered = xf - mean
        var = jnp.mean(centered * centered, axis=-1, keepdims=True)
        scale = lax.rsqrt(var + 1e-05)
        unit = centered * scale
        normed[m] = unit
        rstd[m] = jnp.broadcast_to(scale, rstd.shape[1:])
        hidden[m] = (unit * gain + bias).astype(jnp.bfloat16)

        for piece in range(PIECES):
            for t in range(piece * tiles // PIECES, (piece + 1) * tiles // PIECES):
                part, inside = half_tile(t)
                cols = slice(t * TILE, (t + 1) * TILE)
                u = jnp.dot(hidden[m], weight[part, :, inside], preferred_element_type=F32)
                offset[m, :, cols] = u - lines[1:2, cols]
                square = u * u
                bent = jnp.tanh(SLOPE * (u * (1.0 + CUBIC * square)))
                half = 0.5 * (1.0 + bent)
                slope[m, :, cols] = half + (0.5 * SLOPE) * u * (1.0 - bent * bent) * (
                    1.0 + (3.0 * CUBIC) * square
                )
                leaving[m, :, cols] = (entering[m, :, cols].astype(F32) + u * half).astype(
                    jnp.bfloat16
                )

            @pl.when(section < 3)
            def _():
                onward(m, piece).start()

        return carry

    lax.fori_loop(0, micros, forward, 0)

    def gram(which, rows):
        blocks = width // BLK
        for j in range(2 * 4 * GROUP):
            at = (which, j // (4 * GROUP), j // GROUP % 4, j % GROUP)
            if j >= blocks:
                grams[at] = jnp.eye(BLK, dtype=F32)
                continue
            piece = rows[:, :, j * BLK : (j + 1) * BLK].reshape(micros * mrows, BLK)
            grams[at] = lax.dot_general(
                piece, piece, (((0,), (0,)), ((), ())), preferred_element_type=F32
            )

    ring1 = [me + (wrap4(p1 + d) - p1) * stride1 for d in range(4)]
    ring2 = [me + (wrap4(p2 + d) - p2) * stride2 for d in range(4)]
    place = (core, p1, p2, sibling, ring1, ring2, across)
    a_stages, g_stages = (
        factor_stages(which, place, remote, total, grams, out, buffers, factor_send, factor_recv)
        for which in range(2)
    )

    def run(stages, condition):
        @pl.when(condition)
        def _():
            for stage_ in stages:
                stage_()

    @pl.when(section < 3)
    def _():
        gram(0, hidden)

    run(a_stages[:3], section < 3)
    run(a_stages[3:6], section < 2)
    run(a_stages[6:8], section == 0)

    def backward(m, carry):
        @pl.when(last)
        def _():
            arriving[m] = cotangent[m]

        @pl.when(section < 3)
        def _():
            for piece in range(BACKS):
                back(m, piece).wait_recv()

        gradient[m] = (slope[m] * arriving[m].astype(F32)).astype(jnp.bfloat16)

        @pl.when(section > 0)
        def _():
            du = gradient[m].astype(F32)
            level = jnp.sum(du * lines[0:1], axis=-1, keepdims=True) * (1.0 / width)
            along = jnp.sum(du * offset[m], axis=-1, keepdims=True) * (1.0 / width)
            scale = rstd[m, :, :1]
            for t in range(tiles):
                rows = slice(t * TILE, (t + 1) * TILE)
                dh = sum(
                    lax.dot_general(
                        gradient[m, :, part * side : (part + 1) * side], weight[part, rows, :],
                        (((1,), (1,)), ((), ())), preferred_element_type=F32,
                    )
                    for part in range(2)
                )
                change = scale * (dh * norm_gain[:, rows] - level - normed[m, :, rows] * along)
                returning[m, :, rows] = (arriving[m, :, rows].astype(F32) + change).astype(
                    jnp.bfloat16
                )
                if (t + 1) % (tiles // BACKS) == 0:
                    back(m, t // (tiles // BACKS)).start()

        return carry

    lax.fori_loop(0, micros, backward, 0)

    gram(1, gradient)
    g_stages[0]()

    @pl.when(last)
    def _():
        gram(0, hidden)

    for k in range(8):
        run(a_stages[k : k + 1], last if k < 3 else section >= (2 if k < 6 else 1))
        if k:
            g_stages[k]()
    a_stages[8]()
    g_stages[8]()

    pair.wait_send()
    z_copy.wait_send()
    for item in started + twins:
        item.wait_send()

    def drain(m, carry):
        @pl.when(section < 3)
        def _():
            for piece in range(PIECES):
                onward(m, piece).wait_send()

        @pl.when(section > 0)
        def _():
            for piece in range(BACKS):
                back(m, piece).wait_send()

        return carry

    lax.fori_loop(0, micros, drain, 0)


def per_device(tokens, cotangent, norm_gain, norm_bias, proj_weight):
    rows, width = tokens.shape
    depth = 2 * proj_weight.shape[1]
    mrows = rows // MICRO
    blocks = width // BLK
    shard = proj_weight[0].astype(F32).reshape(depth // 2, 2, width // 2).swapaxes(0, 1)
    by_micro = (MICRO, mrows, width)
    every = (2, 4, GROUP, BLK, BLK)
    vmem = pl.BlockSpec(memory_space=pltpu.VMEM)
    dma = pltpu.SemaphoreType.DMA

    def pair_of(*shape):
        return pltpu.VMEM((2,) + shape, F32)

    inverses = pl.pallas_call(
        functools.partial(pipeline_kernel, float(rows * lax.axis_size("dp"))),
        out_shape=jax.ShapeDtypeStruct((2,) + every, F32),
        in_specs=[vmem] * 5,
        out_specs=vmem,
        scratch_shapes=[
            pair_of(*every),
            pltpu.VMEM((2, width, width // 2), jnp.bfloat16),
            pltpu.VMEM((depth, width // 2), F32),
            pltpu.VMEM(by_micro, jnp.bfloat16),
            pltpu.VMEM(by_micro, jnp.bfloat16),
            pltpu.VMEM(by_micro, jnp.bfloat16),
            pltpu.VMEM(by_micro, F32),
            pltpu.VMEM((MICRO, mrows, BLK), F32),
            pltpu.VMEM(by_micro, F32),
            pltpu.VMEM(by_micro, F32),
            pltpu.VMEM((8, width), F32),
            pltpu.VMEM(by_micro, jnp.bfloat16),
            pltpu.VMEM(by_micro, jnp.bfloat16),
            pltpu.VMEM(by_micro, jnp.bfloat16),
            dma, dma, dma, dma, dma((40,)), dma((40,)), dma((32,)), dma((32,)),
            dma((MICRO, PIECES)), dma((MICRO, PIECES)), dma((MICRO, BACKS)), dma((MICRO, BACKS)),
            dma((2, COPIES)), dma((2, COPIES)),
            pair_of(4, GROUP, BLK, BLK),
            pair_of(4, GROUP, BLK, BLK),
            pair_of(3, GROUP, BLK, BLK),
            pair_of(3, GROUP, BLK // 4, BLK),
            pair_of(GROUP, BLK // 4, BLK),
            pair_of(GROUP, BLK // 4, BLK),
            pair_of(GROUP, BLK, BLK),
            pair_of(GROUP, BLK, BLK),
        ],
        compiler_params=pltpu.CompilerParams(
            collective_id=0, has_side_effects=True, vmem_limit_bytes=56 * 1024 * 1024
        ),
    )(tokens.reshape(by_micro), cotangent.reshape(by_micro), norm_gain, norm_bias, shard)
    inverses = inverses.reshape(2, 8 * GROUP, BLK, BLK)[:, :blocks]
    return (inverses[:1], inverses[1:])


def solution(mesh):
    in_specs = (
        P("dp", None),
        P("dp", None),
        P("pipe", None),
        P("pipe", None),
        P("pipe", "dp", None),
    )
    out_specs = (P("pipe", None, None, None), P("pipe", None, None, None))
    return jax.shard_map(
        per_device, mesh=mesh, in_specs=in_specs, out_specs=out_specs, check_vma=False
    )
```
